1024 devices in a mesh: pole: 16 (over y_hi, z), row: 16 (over x, core), col: 4 (over y_lo).
Axes of the slice: x: 8, y: 8 (y_hi: 2, y_lo: 4; y = y_hi * 4 + y_lo), z: 8, core: 2. Of those that a mesh axis runs over, the one named last changes fastest.
Arguments:
- hamiltonian: float32 [4096, 256], P(('row', 'col')), may hold values from -6 to 6
- margin: float32 [4096, 256], P(('row', 'col')), may hold values from -3 to 3
- owner: int32 [4096], P(('row', 'col')), may hold values from 0 to 4095, as said below
- inverse_blocks: float32 [16, 2, 4096, 4096], P('pole', None, 'col', 'row'), may hold values from -0.125 to 0.125
- pole_index: int32 [16], P('pole'), may hold values from 0 to 63
Outputs:
- density: float32 [4096, 256], P(('col', 'row', 'pole'))
The draws below stay inside these ranges and needn't reach their ends.
Inputs may be any that keep to these rules, and one draw needn't show every extreme that they name: `owner`: A permutation of the 4096 supernodal rows; among the orbital rows of one device along row+col at most 8 have owners in one block of 256 consecutive supernodal rows, and some device reaches 8 for every block.
All inputs are finite; a program needn't handle non-finite values.
Results may differ from the reference program's by a relative error of at most 0.0001.
Values sent between devices are 32-bit elements; how exact they have to be, the bound alone decides.
No kernel may reach another device: no remote copies, remote signals or barrier semaphores. Data moves between devices by JAX's collectives and lax.ppermute only.
A program may use at most 32 MiB of HBM per device.

```python
import math
import jax
import jax.numpy as jnp
from jax import lax

POLES = 64
NA = 4096
NK = 256
N_POLE = 16
N_ROW = 16
N_COL = 4


def draw_owner(key, part):
    key = jax.random.fold_in(key, 11)
    senders = N_ROW * N_COL
    block_rows = NA // N_ROW
    share_rows = NA // senders
    average = share_rows // N_ROW
    key_levels, key_pattern, key_blocks, key_shuffle = jax.random.split(key, 4)
    levels = jax.random.randint(key_levels, (N_ROW // 2,), 0, average + 1).at[0].set(average)
    pattern = jnp.stack([levels, -levels], axis=1).reshape(N_ROW)
    pattern = pattern[jax.random.permutation(key_pattern, N_ROW)]
    sender_ids = jnp.arange(senders)
    target_ids = jnp.arange(N_ROW)
    counts = average + pattern[(sender_ids[:, None] + target_ids[None, :]) % N_ROW]
    limits = jnp.cumsum(counts, axis=1)
    positions = jnp.arange(share_rows)
    destination = jnp.sum((limits[:, None, :] <= positions[None, :, None]).astype(jnp.int32), axis=2)
    starts = limits - counts
    ranking = positions[None, :] - jnp.take_along_axis(starts, destination, axis=1)
    before = jnp.cumsum(counts, axis=0) - counts
    placed = jnp.take_along_axis(before, destination, axis=1) + ranking
    shuffles = jax.vmap(lambda single: jax.random.permutation(single, block_rows))(jax.random.split(key_blocks, N_ROW))
    result = destination * block_rows + shuffles[destination, placed]
    shuffle_order = jax.vmap(lambda single: jax.random.permutation(single, share_rows))(jax.random.split(key_shuffle, senders))
    result = jnp.take_along_axis(result, shuffle_order, axis=1)
    return result.reshape(NA).astype(jnp.int32)


def with_ends(entries, own_key, least, top_value):
    longest = entries.shape.index(max(entries.shape))
    spots = []
    for shift in (0, 1):
        where = [jax.random.randint(jax.random.fold_in(own_key, axis), (), 0, length) for axis, length in enumerate(entries.shape)]
        where[longest] = (where[longest] + shift) % entries.shape[longest]
        spots.append(tuple(where))
    return entries.at[spots[0]].set(least).at[spots[1]].set(top_value)


def strengthened(drawn, rng, source, target, shards_of, factor):
    owner, partner = [(jnp.arange(drawn.shape[position]) // (drawn.shape[position] // shards_of)).reshape([-1 if axis == position else 1 for axis in range(drawn.ndim)]) for position in (source, target)]
    chosen = jax.random.permutation(rng, shards_of)[partner]
    strong = (owner == chosen) | (owner == (partner + shards_of // 2) % shards_of)
    return jnp.where(strong, factor * drawn, drawn)


def shard_levels(stream_key, shape, shards, least, top_value):
    loudness, own = 1.0, jax.random.fold_in(stream_key, 6)
    for position, shards_of in shards:
        steps = jnp.exp(jax.random.uniform(jax.random.fold_in(own, position), (shards_of,), jnp.float32, least / len(shards), top_value / len(shards)))
        loudness = loudness * jnp.repeat(steps, shape[position] // shards_of).reshape([-1 if axis == position else 1 for axis in range(len(shape))])
    return loudness


def scatter_about(stream_key, extent, width, reach, pieces=(), held_as=jnp.bfloat16):
    values = jax.random.normal(stream_key, extent, jnp.float32) * width
    if len(pieces) > 0:
        values = shard_levels(stream_key, extent, pieces, -0.22, 0.18) * values
    return jnp.clip(values, min=-reach, max=reach).astype(held_as)


def gaussian_with(key, extent, width, reach, cuts, heavy, dtype=jnp.bfloat16):
    values = width * jax.random.normal(key, extent, jnp.float32)
    if cuts:
        values = values * shard_levels(key, extent, cuts, -0.22, 0.18)
    return jnp.clip(strengthened(values, jax.random.fold_in(key, 3), *heavy), -reach, reach).astype(dtype)


def setup_inputs(seed: int = 0) -> dict:
    streams_of = jax.random.split(jax.random.key(seed), 6)
    return {
        "hamiltonian": scatter_about(streams_of[0], (NA, NK), 1.0, 6.0, ((0, 64),), jnp.float32),
        "margin": scatter_about(streams_of[1], (NA, NK), 0.5, 3.0, ((0, 64),), jnp.float32),
        "owner": draw_owner(jax.random.fold_in(streams_of[5], 71), 0),
        "inverse_blocks": gaussian_with(streams_of[3], (N_POLE, 2, NA, NA), NA ** -0.5, 0.125, ((0, 16), (2, 4), (3, 16)), (3, 2, 16, 2.0), jnp.float32),
        "pole_index": with_ends(jax.random.randint(streams_of[4], (N_POLE,), 0, POLES), jax.random.fold_in(streams_of[4], 1), 0, POLES - 1).astype(jnp.int32),
    }


pole_radius = 1.5
weight_scale = 0.3


def reference(hamiltonian, margin, owner, inverse_blocks, pole_index):
    ham_rows = jnp.zeros_like(hamiltonian).at[owner].set(hamiltonian)
    ovl_rows = jnp.zeros_like(margin).at[owner].set(margin)

    def one_pole(total, inputs):
        blocks, pole_level = inputs
        theta_pole = math.pi * (pole_level.astype(jnp.float32) + 0.5) / POLES
        energy = pole_radius * jnp.cos(theta_pole)
        damping = pole_radius * jnp.sin(theta_pole)
        weight_re = weight_scale * jnp.cos(theta_pole)
        weight_im = weight_scale * jnp.sin(theta_pole)
        panel_re = ham_rows - energy * ovl_rows
        panel_im = -damping * ovl_rows
        high = lax.Precision.HIGHEST
        real_part = -(jnp.dot(blocks[0], panel_re, precision=high) - jnp.dot(blocks[1], panel_im, precision=high))
        imag_part = -(jnp.dot(blocks[0], panel_im, precision=high) + jnp.dot(blocks[1], panel_re, precision=high))
        return total + weight_re * imag_part + weight_im * real_part, None

    start_total = jnp.zeros((NA, NK), jnp.float32)
    density, unused = lax.scan(one_pole, start_total, (inverse_blocks, pole_index))
    return density
```

```python
import math

import jax
import jax.numpy as jnp
from jax import lax
from jax.experimental import pallas as pl
from jax.experimental.pallas import tpu as pltpu
from jax.sharding import Mesh, PartitionSpec as P

POLES = 64
pole_radius = 1.5
weight_scale = 0.3

LANES = 128
SLOTS = 8
VMEM = pl.BlockSpec(memory_space=pltpu.VMEM)
SMEM = pl.BlockSpec(memory_space=pltpu.SMEM)
PARAMS = pltpu.CompilerParams(vmem_limit_bytes=40 * 1024 * 1024)


def iota(shape, axis):
    return lax.broadcasted_iota(jnp.int32, shape, axis)


def pack_kernel(rows_axis, cols_axis, ham_ref, mar_ref, owner_ref, out_ref):
    share, width = ham_ref.shape
    shift = (4096 // rows_axis).bit_length() - 1
    own_r = jnp.broadcast_to(owner_ref[...].astype(jnp.float32), (share, share))
    own_c = jnp.sum(jnp.where(iota((share, share), 0) == iota((share, share), 1), own_r, 0.0), axis=1, keepdims=True)
    own_c = jnp.broadcast_to(own_c, (share, share)).astype(jnp.int32)
    own_r = own_r.astype(jnp.int32)
    same = (own_r >> shift) == (own_c >> shift)
    first, second = iota((share, share), 0), iota((share, share), 1)
    rank_r = jnp.sum(jnp.where(same & (first < second), 1.0, 0.0), axis=0, keepdims=True)
    rank_c = jnp.sum(jnp.where(same & (second < first), 1.0, 0.0), axis=1, keepdims=True)
    slot_r = (own_r[:1] >> shift) * SLOTS + rank_r.astype(jnp.int32)
    slot_c = (own_c[:, :1] >> shift) * SLOTS + rank_c.astype(jnp.int32)
    total = rows_axis * SLOTS
    packer = jnp.where(iota((total, share), 0) == jnp.broadcast_to(slot_r, (total, share)), 1.0, 0.0)
    within = (own_c[:, :1] & ((1 << shift) - 1)) + 1
    labels = jnp.where(
        iota((share, total), 1) == jnp.broadcast_to(slot_c, (share, total)),
        jnp.broadcast_to(within, (share, total)).astype(jnp.float32),
        0.0,
    )
    labels = jnp.sum(labels, axis=0, keepdims=True)
    chunk = 2 * width // LANES * SLOTS + 1
    for which, ref in enumerate((ham_ref, mar_ref)):
        packed = jnp.dot(packer, ref[...], precision=lax.Precision.HIGHEST, preferred_element_type=jnp.float32)
        for part in range(width // LANES):
            offset = (which * (width // LANES) + part) * SLOTS
            for row in range(rows_axis):
                tile = packed[row * SLOTS : (row + 1) * SLOTS, part * LANES : (part + 1) * LANES]
                for col in range(cols_axis):
                    base = (row * cols_axis + col) * chunk + offset
                    out_ref[base : base + SLOTS, :] = tile
    for target in range(rows_axis * cols_axis):
        base = (target + 1) * chunk - 1
        out_ref[base : base + 1, :] = labels


def split(value):
    high = value.astype(jnp.bfloat16)
    return high, (value - high.astype(jnp.float32)).astype(jnp.bfloat16)


def coefficient_kernel(coef_ref, blocks_ref, high_ref, low_ref):
    rows, depth = blocks_ref.shape[1:]
    piece = rows // 16
    for index in range(16):
        x, core = divmod(index, 2)
        re = blocks_ref[0, index * piece : (index + 1) * piece, :]
        im = blocks_ref[1, index * piece : (index + 1) * piece, :]
        for which in range(2):
            high, low = split(coef_ref[2 * which] * re + coef_ref[2 * which + 1] * im)
            at = (core, slice(x * piece, (x + 1) * piece), slice(which * depth, (which + 1) * depth))
            high_ref[at] = high
            low_ref[at] = low


def product(high, low, panel_high, panel_low):
    dot = lambda a, b: jnp.dot(a, b, preferred_element_type=jnp.float32)
    return dot(high, panel_high) + (dot(low, panel_high) + dot(high, panel_low))


def store_chunks(out_ref, value):
    pairs = value.shape[0] // 8
    left = value[:, :LANES].reshape(pairs, 8, LANES)
    right = value[:, LANES:].reshape(pairs, 8, LANES)
    upper = iota((pairs, 8, LANES), 1) < 4
    out_ref[:, 0] = jnp.where(upper, left, pltpu.roll(right, 4, 1))
    out_ref[:, 1] = jnp.where(upper, pltpu.roll(left, 4, 1), right)


def first_kernel(senders, place_ref, rows_ref, high_ref, low_ref, out_ref, panel_high_ref, panel_low_ref):
    row, core = place_ref[0], place_ref[1]
    chunk = rows_ref.shape[0] // senders
    depth = panel_high_ref.shape[0] // 2
    parts = (chunk - 1) // SLOTS
    labels = rows_ref[pl.ds(chunk - 1, senders, stride=chunk), :]
    lane = iota((senders, LANES), 1)
    wanted = (iota((senders, depth), 1) + 1).astype(jnp.float32)
    places = []
    for slot in range(SLOTS):
        label = jnp.sum(jnp.where(lane == row * SLOTS + slot, labels, 0.0), axis=1, keepdims=True)
        places.append(jnp.where(jnp.broadcast_to(label, (senders, depth)) == wanted, 1.0, 0.0))
    places = jnp.concatenate(places, axis=0).astype(jnp.bfloat16)
    for part in range(parts):
        values = [rows_ref[pl.ds(part * SLOTS + slot, senders, stride=chunk), :] for slot in range(SLOTS)]
        pieces = split(jnp.concatenate(values, axis=0))
        which, left = divmod(part, parts // 2)
        at = (slice(which * depth, (which + 1) * depth), slice(left * LANES, (left + 1) * LANES))
        for ref, piece in zip((panel_high_ref, panel_low_ref), pieces):
            placed = lax.dot_general(places, piece, (((0,), (0,)), ((), ())), preferred_element_type=jnp.float32)
            ref[at] = placed.astype(jnp.bfloat16)
    other = 1 - core
    store_chunks(out_ref, product(high_ref[other], low_ref[other], panel_high_ref[...], panel_low_ref[...]))


def second_kernel(place_ref, high_ref, low_ref, panel_high_ref, panel_low_ref, out_ref):
    core = place_ref[1]
    store_chunks(out_ref, product(high_ref[core], low_ref[core], panel_high_ref[...], panel_low_ref[...]))


def last_kernel(parts_ref, out_ref):
    total = jnp.sum(parts_ref[...], axis=0)
    out_ref[:, :LANES] = total[:4]
    out_ref[:, LANES:] = total[4:]


def per_device(hamiltonian, margin, owner, inverse_blocks, pole_index):
    rows_axis = lax.axis_size("x") * lax.axis_size("core")
    cols_axis = lax.axis_size("yl")
    share, width = hamiltonian.shape
    senders = rows_axis * cols_axis
    chunk = 2 * width // LANES * SLOTS + 1
    packed = pl.pallas_call(
        lambda *refs: pack_kernel(rows_axis, cols_axis, *refs),
        out_shape=jax.ShapeDtypeStruct((senders * chunk, LANES), jnp.float32),
        in_specs=[VMEM] * 3,
        out_specs=VMEM,
        compiler_params=PARAMS,
        name="pack_rows",
    )(hamiltonian, margin, owner.reshape(1, share))
    arrived = lax.all_to_all(
        packed.reshape(senders, 1, chunk * LANES), ("x", "core", "yl"), split_axis=0, concat_axis=0, tiled=True
    ).reshape(senders * chunk, LANES)

    theta = math.pi * (pole_index[0].astype(jnp.float32) + 0.5) / POLES
    energy, damping = pole_radius * jnp.cos(theta), pole_radius * jnp.sin(theta)
    weight_re, weight_im = weight_scale * jnp.cos(theta), weight_scale * jnp.sin(theta)
    shifted_re = weight_re * energy - weight_im * damping
    shifted_im = weight_re * damping + weight_im * energy
    coefs = jnp.stack([-weight_im, -weight_re, shifted_im, shifted_re])
    block_rows, depth = inverse_blocks.shape[2:]
    half = jax.ShapeDtypeStruct((2, block_rows // 2, 2 * depth), jnp.bfloat16)
    high, low = pl.pallas_call(
        coefficient_kernel,
        out_shape=(half, half),
        in_specs=[SMEM, VMEM],
        out_specs=(VMEM, VMEM),
        compiler_params=PARAMS,
        cost_estimate=pl.CostEstimate(flops=4 * block_rows * depth, bytes_accessed=16 * block_rows * depth, transcendentals=0),
        name="left_factors",
    )(coefs, inverse_blocks[0])

    core = lax.axis_index("core")
    place = jnp.stack([lax.axis_index("x") * lax.axis_size("core") + core, core]).astype(jnp.int32)
    chunks = jax.ShapeDtypeStruct((block_rows // 16, 2, 8, LANES), jnp.float32)
    panel = jax.ShapeDtypeStruct((2 * depth, width), jnp.bfloat16)
    sent, panel_high, panel_low = pl.pallas_call(
        lambda *refs: first_kernel(senders, *refs),
        out_shape=(chunks, panel, panel),
        in_specs=[SMEM] + [VMEM] * 3,
        out_specs=(VMEM,) * 3,
        compiler_params=PARAMS,
        name="place_and_multiply",
    )(place, arrived, high, low)
    received = lax.ppermute(sent, "core", [(0, 1), (1, 0)])
    kept = pl.pallas_call(
        second_kernel,
        out_shape=chunks,
        in_specs=[SMEM] + [VMEM] * 4,
        out_specs=VMEM,
        compiler_params=PARAMS,
        cost_estimate=pl.CostEstimate(flops=3 * 2 * block_rows * depth * width, bytes_accessed=2 * block_rows * depth * 4, transcendentals=0),
        name="multiply_own",
    )(place, high, low, panel_high, panel_low)
    both = (kept + received).reshape(block_rows // 8, 8, LANES)
    parts = lax.all_to_all(both, ("x", "yh", "z"), split_axis=0, concat_axis=0, tiled=True)
    return pl.pallas_call(
        last_kernel,
        out_shape=jax.ShapeDtypeStruct((4, width), jnp.float32),
        in_specs=[VMEM],
        out_specs=VMEM,
        compiler_params=PARAMS,
        name="sum_parts",
    )(parts)


def solution(mesh):
    fine = Mesh(mesh.devices.reshape(2, 8, 8, 2, 4), ("yh", "z", "x", "core", "yl"))
    in_specs = (
        P(("x", "core", "yl"), None),
        P(("x", "core", "yl"), None),
        P(("x", "core", "yl")),
        P(("yh", "z"), None, "yl", ("x", "core")),
        P(("yh", "z")),
    )
    out_specs = P(("yl", "x", "core", "yh", "z"), None)
    return jax.shard_map(per_device, mesh=fine, in_specs=in_specs, out_specs=out_specs, check_vma=False)
```

```python
import math

import jax
import jax.numpy as jnp
from jax import lax
from jax.experimental import pallas as pl
from jax.experimental.pallas import tpu as pltpu
from jax.sharding import Mesh, PartitionSpec as P

POLES = 64
pole_radius = 1.5
weight_scale = 0.3

LANES = 128
SLOTS = 8
CHUNK = 2 * SLOTS + 1
VMEM = pl.BlockSpec(memory_space=pltpu.VMEM)
SMEM = pl.BlockSpec(memory_space=pltpu.SMEM)
HBM = pl.BlockSpec(memory_space=pltpu.HBM)
PARAMS = pltpu.CompilerParams(vmem_limit_bytes=40 * 1024 * 1024)


def iota(shape, axis):
    return lax.broadcasted_iota(jnp.int32, shape, axis)


def pack_kernel(rows_axis, cols_axis, shift, place_ref, ham_ref, mar_ref, owner_ref, out_ref, ham, mar, owner, sems):
    share = ham.shape[0]
    columns = pl.ds(pl.multiple_of(place_ref[2] * LANES, LANES), LANES)
    copies = [
        pltpu.make_async_copy(owner_ref, owner, sems.at[0]),
        pltpu.make_async_copy(ham_ref.at[:, columns], ham, sems.at[1]),
        pltpu.make_async_copy(mar_ref.at[:, columns], mar, sems.at[2]),
    ]
    for copy in copies:
        copy.start()
    copies[0].wait()
    own_r = jnp.broadcast_to(owner[...].astype(jnp.float32), (share, share))
    own_c = jnp.sum(jnp.where(iota((share, share), 0) == iota((share, share), 1), own_r, 0.0), axis=1, keepdims=True)
    own_c = jnp.broadcast_to(own_c, (share, share)).astype(jnp.int32)
    own_r = own_r.astype(jnp.int32)
    same = (own_r >> shift) == (own_c >> shift)
    first, second = iota((share, share), 0), iota((share, share), 1)
    rank_r = jnp.sum(jnp.where(same & (first < second), 1.0, 0.0), axis=0, keepdims=True)
    rank_c = jnp.sum(jnp.where(same & (second < first), 1.0, 0.0), axis=1, keepdims=True)
    slot_r = (own_r[:1] >> shift) * SLOTS + rank_r.astype(jnp.int32)
    slot_c = (own_c[:, :1] >> shift) * SLOTS + rank_c.astype(jnp.int32)
    total = rows_axis * SLOTS
    packer = jnp.where(iota((total, share), 0) == jnp.broadcast_to(slot_r, (total, share)), 1.0, 0.0)
    within = (own_c[:, :1] & ((1 << shift) - 1)) + 1
    labels = jnp.where(
        iota((share, total), 1) == jnp.broadcast_to(slot_c, (share, total)),
        jnp.broadcast_to(within, (share, total)).astype(jnp.float32),
        0.0,
    )
    labels = jnp.sum(labels, axis=0, keepdims=True)
    for target in range(rows_axis * cols_axis):
        base = (target + 1) * CHUNK - 1
        out_ref[base : base + 1, :] = labels
    for which, ref in enumerate((ham, mar)):
        copies[1 + which].wait()
        packed = jnp.dot(packer, ref[...], precision=lax.Precision.HIGHEST, preferred_element_type=jnp.float32)
        for row in range(rows_axis):
            tile = packed[row * SLOTS : (row + 1) * SLOTS]
            for col in range(cols_axis):
                base = (row * cols_axis + col) * CHUNK + which * SLOTS
                out_ref[base : base + SLOTS, :] = tile


def split(value):
    high = value.astype(jnp.bfloat16)
    return high, (value - high.astype(jnp.float32)).astype(jnp.bfloat16)


def coefficient_kernel(pieces, coef_ref, blocks_ref, first_ref, second_ref, blocks, sems):
    rows, depth = blocks.shape[1:]
    piece = rows // pieces
    half = piece // 2
    copies = []
    for x in range(pieces):
        at = pl.ds(x * piece, piece)
        copies.append(pltpu.make_async_copy(blocks_ref.at[:, at], blocks.at[:, at], sems.at[x]))
        copies[-1].start()
    for x in range(pieces):
        copies[x].wait()
        for core, ref in enumerate((first_ref, second_ref)):
            at = slice(x * piece + core * half, x * piece + (core + 1) * half)
            re, im = blocks[0, at, :], blocks[1, at, :]
            for which in range(2):
                value = coef_ref[2 * which] * re + coef_ref[2 * which + 1] * im
                ref[x * half : (x + 1) * half, which * depth : (which + 1) * depth] = value


def combine_kernel(own_ref, other_ref, high_ref, low_ref):
    for at in range(0, own_ref.shape[0], 64):
        rows = slice(at, at + 64)
        high_ref[rows], low_ref[rows] = split(own_ref[rows] + other_ref[rows])


def product(high, low, panel):
    both = jnp.dot(high, panel, preferred_element_type=jnp.float32)
    return both[:, :LANES] + (both[:, LANES:] + jnp.dot(low, panel[:, :LANES], preferred_element_type=jnp.float32))


def multiply(first, out_ref, which, highs, lows, panel_ref):
    for index in range(2):

        @pl.when(which == index)
        def _():
            out_ref[...] = product(highs[index][...], lows[index][...], panel_ref[...])


def first_kernel(senders, place_ref, rows_ref, high0, low0, high1, low1, out_ref, panel_ref):
    row, core = place_ref[0], place_ref[1]
    depth = panel_ref.shape[0] // 2
    labels = rows_ref[pl.ds(CHUNK - 1, senders, stride=CHUNK), :]
    lane = iota((senders, LANES), 1)
    wanted = (iota((senders, depth), 1) + 1).astype(jnp.float32)
    places = []
    for slot in range(SLOTS):
        label = jnp.sum(jnp.where(lane == row * SLOTS + slot, labels, 0.0), axis=1, keepdims=True)
        places.append(jnp.where(jnp.broadcast_to(label, (senders, depth)) == wanted, 1.0, 0.0))
    places = jnp.concatenate(places, axis=0).astype(jnp.bfloat16)
    for which in range(2):
        values = [rows_ref[pl.ds(which * SLOTS + slot, senders, stride=CHUNK), :] for slot in range(SLOTS)]
        pieces = jnp.concatenate(split(jnp.concatenate(values, axis=0)), axis=1)
        placed = lax.dot_general(places, pieces, (((0,), (0,)), ((), ())), preferred_element_type=jnp.float32)
        panel_ref[which * depth : (which + 1) * depth, :] = placed.astype(jnp.bfloat16)
    multiply(True, out_ref, 1 - core, (high0, high1), (low0, low1), panel_ref)


def second_kernel(place_ref, high0, low0, high1, low1, panel_ref, out_ref):
    multiply(False, out_ref, place_ref[1], (high0, high1), (low0, low1), panel_ref)


def last_kernel(parts_ref, out_ref):
    total = jnp.sum(parts_ref[...].reshape(-1, 8, LANES), axis=0)
    out_ref[:, :LANES] = total[:4]
    out_ref[:, LANES:] = total[4:]


def per_device(hamiltonian, margin, owner, inverse_blocks, pole_index):
    rows_axis = lax.axis_size("x") * lax.axis_size("core")
    cols_axis = lax.axis_size("yl")
    z_axis = lax.axis_size("z")
    share, width = hamiltonian.shape
    block_rows, depth = inverse_blocks.shape[2:]
    senders = rows_axis * cols_axis
    core = lax.axis_index("core")
    row = lax.axis_index("x") * lax.axis_size("core") + core
    place = jnp.stack([row, core, lax.axis_index("z") % 2]).astype(jnp.int32)
    packed = pl.pallas_call(
        lambda *refs: pack_kernel(rows_axis, cols_axis, depth.bit_length() - 1, *refs),
        out_shape=jax.ShapeDtypeStruct((senders * CHUNK, LANES), jnp.float32),
        in_specs=[SMEM, HBM, HBM, HBM],
        out_specs=VMEM,
        scratch_shapes=[
            pltpu.VMEM((share, LANES), jnp.float32),
            pltpu.VMEM((share, LANES), jnp.float32),
            pltpu.VMEM((1, share), jnp.int32),
            pltpu.SemaphoreType.DMA((3,)),
        ],
        compiler_params=PARAMS,
        name="pack_rows",
    )(place, hamiltonian, margin, owner.reshape(1, share))
    arrived = lax.all_to_all(
        packed.reshape(senders, 1, CHUNK * LANES), ("x", "core", "yl"), split_axis=0, concat_axis=0, tiled=True
    ).reshape(senders * CHUNK, LANES)

    theta = math.pi * (pole_index[0].astype(jnp.float32) + 0.5) / POLES
    energy, damping = pole_radius * jnp.cos(theta), pole_radius * jnp.sin(theta)
    weight_re, weight_im = weight_scale * jnp.cos(theta), weight_scale * jnp.sin(theta)
    shifted_re = weight_re * energy - weight_im * damping
    shifted_im = weight_re * damping + weight_im * energy
    coefs = jnp.stack([-weight_im, -weight_re, shifted_im, shifted_re])
    pieces = lax.axis_size("x")
    factor = jax.ShapeDtypeStruct((block_rows // 2, 2 * depth), jnp.float32)
    factors = pl.pallas_call(
        lambda *refs: coefficient_kernel(pieces, *refs),
        out_shape=(factor, factor),
        in_specs=[SMEM, HBM],
        out_specs=(VMEM, VMEM),
        scratch_shapes=[pltpu.VMEM((2, block_rows, depth), jnp.float32), pltpu.SemaphoreType.DMA((pieces,))],
        compiler_params=PARAMS,
        cost_estimate=pl.CostEstimate(flops=6 * block_rows * depth, bytes_accessed=16 * block_rows * depth, transcendentals=0),
        name="left_factors",
    )(coefs, inverse_blocks[0])
    pairs = (
        [(i, i ^ 1) for i in range(z_axis)],
        [(i, (i - 1 if i % 2 == 0 else i + 1) % z_axis) for i in range(z_axis)],
    )
    others = [lax.ppermute(own, "z", pair) for own, pair in zip(factors, pairs)]
    part = jax.ShapeDtypeStruct(factor.shape, jnp.bfloat16)
    summed = []
    for own, other in zip(factors, others):
        summed += pl.pallas_call(
            combine_kernel,
            out_shape=(part, part),
            in_specs=[VMEM] * 2,
            out_specs=(VMEM, VMEM),
            compiler_params=PARAMS,
            cost_estimate=pl.CostEstimate(flops=block_rows * depth * 3, bytes_accessed=12 * block_rows * depth, transcendentals=0),
            name="pair_sums",
        )(own, other)

    chunks = jax.ShapeDtypeStruct((block_rows // 2, LANES), jnp.float32)
    sent, panel = pl.pallas_call(
        lambda *refs: first_kernel(senders, *refs),
        out_shape=(chunks, jax.ShapeDtypeStruct((2 * depth, 2 * LANES), jnp.bfloat16)),
        in_specs=[SMEM] + [VMEM] * 5,
        out_specs=(VMEM,) * 2,
        compiler_params=PARAMS,
        name="place_and_multiply",
    )(place, arrived, *summed)
    received = lax.ppermute(sent, "core", [(0, 1), (1, 0)])
    kept = pl.pallas_call(
        second_kernel,
        out_shape=chunks,
        in_specs=[SMEM] + [VMEM] * 5,
        out_specs=VMEM,
        compiler_params=PARAMS,
        cost_estimate=pl.CostEstimate(flops=3 * block_rows * 2 * depth * LANES, bytes_accessed=4 * block_rows * depth, transcendentals=0),
        name="multiply_own",
    )(place, *summed, panel)
    both = (kept + received).reshape(block_rows // 8, 4, LANES)
    parts = lax.all_to_all(both, ("x", "yh", "z"), split_axis=0, concat_axis=0, tiled=True)
    return pl.pallas_call(
        last_kernel,
        out_shape=jax.ShapeDtypeStruct((4, width), jnp.float32),
        in_specs=[VMEM],
        out_specs=VMEM,
        compiler_params=PARAMS,
        name="sum_parts",
    )(parts.reshape(block_rows // 2, LANES))


def solution(mesh):
    fine = Mesh(mesh.devices.reshape(2, 8, 8, 2, 4), ("yh", "z", "x", "core", "yl"))
    in_specs = (
        P(("x", "core", "yl"), None),
        P(("x", "core", "yl"), None),
        P(("x", "core", "yl")),
        P(("yh", "z"), None, "yl", ("x", "core")),
        P(("yh", "z")),
    )
    out_specs = P(("yl", "x", "core", "yh", "z"), None)
    return jax.shard_map(per_device, mesh=fine, in_specs=in_specs, out_specs=out_specs, check_vma=False)
```

```python
import math

import jax
import jax.numpy as jnp
from jax import lax
from jax.experimental import pallas as pl
from jax.experimental.pallas import tpu as pltpu
from jax.sharding import Mesh, PartitionSpec as P

POLES = 64
pole_radius = 1.5
weight_scale = 0.3

LANES = 128
SLOTS = 8
CHUNK = 2 * SLOTS + 1
VMEM = pl.BlockSpec(memory_space=pltpu.VMEM)
SMEM = pl.BlockSpec(memory_space=pltpu.SMEM)
HBM = pl.BlockSpec(memory_space=pltpu.HBM)
PREPARE = pltpu.CompilerParams(vmem_limit_bytes=50 * 1024 * 1024)
PARAMS = pltpu.CompilerParams(vmem_limit_bytes=40 * 1024 * 1024)


def iota(shape, axis):
    return lax.broadcasted_iota(jnp.int32, shape, axis)


def prepare_kernel(rows_axis, cols_axis, pieces, place_ref, coef_ref, ham_ref, mar_ref, owner_ref, blocks_ref, *rest):
    out_ref, first_ref, second_ref, ham, mar, owner, blocks, sems = rest
    share = ham.shape[0]
    rows, depth = blocks.shape[1:]
    shift = depth.bit_length() - 1
    columns = pl.ds(pl.multiple_of(place_ref[2] * LANES, LANES), LANES)
    copies = [
        pltpu.make_async_copy(owner_ref, owner, sems.at[0]),
        pltpu.make_async_copy(ham_ref.at[:, columns], ham, sems.at[1]),
        pltpu.make_async_copy(mar_ref.at[:, columns], mar, sems.at[2]),
    ]
    piece = rows // pieces
    for x in range(pieces):
        at = pl.ds(x * piece, piece)
        copies.append(pltpu.make_async_copy(blocks_ref.at[:, at], blocks.at[:, at], sems.at[3 + x]))
    for copy in copies:
        copy.start()
    copies[0].wait()
    own_r = jnp.broadcast_to(owner[...].astype(jnp.float32), (share, share))
    own_c = jnp.sum(jnp.where(iota((share, share), 0) == iota((share, share), 1), own_r, 0.0), axis=1, keepdims=True)
    own_c = jnp.broadcast_to(own_c, (share, share)).astype(jnp.int32)
    own_r = own_r.astype(jnp.int32)
    same = (own_r >> shift) == (own_c >> shift)
    first, second = iota((share, share), 0), iota((share, share), 1)
    rank_r = jnp.sum(jnp.where(same & (first < second), 1.0, 0.0), axis=0, keepdims=True)
    rank_c = jnp.sum(jnp.where(same & (second < first), 1.0, 0.0), axis=1, keepdims=True)
    slot_r = (own_r[:1] >> shift) * SLOTS + rank_r.astype(jnp.int32)
    slot_c = (own_c[:, :1] >> shift) * SLOTS + rank_c.astype(jnp.int32)
    total = rows_axis * SLOTS
    packer = jnp.where(iota((total, share), 0) == jnp.broadcast_to(slot_r, (total, share)), 1.0, 0.0)
    within = (own_c[:, :1] & ((1 << shift) - 1)) + 1
    labels = jnp.where(
        iota((share, total), 1) == jnp.broadcast_to(slot_c, (share, total)),
        jnp.broadcast_to(within, (share, total)).astype(jnp.float32),
        0.0,
    )
    labels = jnp.sum(labels, axis=0, keepdims=True)
    for target in range(rows_axis * cols_axis):
        base = (target + 1) * CHUNK - 1
        out_ref[base : base + 1, :] = labels
    for which, ref in enumerate((ham, mar)):
        copies[1 + which].wait()
        packed = jnp.dot(packer, ref[...], precision=lax.Precision.HIGHEST, preferred_element_type=jnp.float32)
        for row in range(rows_axis):
            tile = packed[row * SLOTS : (row + 1) * SLOTS]
            for col in range(cols_axis):
                base = (row * cols_axis + col) * CHUNK + which * SLOTS
                out_ref[base : base + SLOTS, :] = tile
    half = piece // 2
    for x in range(pieces):
        copies[3 + x].wait()
        for core, ref in enumerate((first_ref, second_ref)):
            at = slice(x * piece + core * half, x * piece + (core + 1) * half)
            re, im = blocks[0, at, :], blocks[1, at, :]
            for which in range(2):
                value = coef_ref[2 * which] * re + coef_ref[2 * which + 1] * im
                ref[x * half : (x + 1) * half, which * depth : (which + 1) * depth] = value


def split(value):
    high = value.astype(jnp.bfloat16)
    return high, (value - high.astype(jnp.float32)).astype(jnp.bfloat16)


def multiply(out_ref, which, owns, others, panel_ref):
    panel = panel_ref[...]
    for index in range(2):

        @pl.when(which == index)
        def _():
            high, low = split(owns[index][...] + others[index][...])
            both = jnp.dot(high, panel, preferred_element_type=jnp.float32)
            more = jnp.dot(low, panel[:, :LANES], preferred_element_type=jnp.float32)
            out_ref[...] = both[:, :LANES] + (both[:, LANES:] + more)


def first_kernel(senders, place_ref, rows_ref, own0, other0, own1, other1, out_ref, panel_ref):
    row, core = place_ref[0], place_ref[1]
    depth = panel_ref.shape[0] // 2
    labels = rows_ref[pl.ds(CHUNK - 1, senders, stride=CHUNK), :]
    lane = iota((senders, LANES), 1)
    wanted = (iota((senders, depth), 1) + 1).astype(jnp.float32)
    places = []
    for slot in range(SLOTS):
        label = jnp.sum(jnp.where(lane == row * SLOTS + slot, labels, 0.0), axis=1, keepdims=True)
        places.append(jnp.where(jnp.broadcast_to(label, (senders, depth)) == wanted, 1.0, 0.0))
    places = jnp.concatenate(places, axis=0).astype(jnp.bfloat16)
    for which in range(2):
        values = [rows_ref[pl.ds(which * SLOTS + slot, senders, stride=CHUNK), :] for slot in range(SLOTS)]
        pieces = jnp.concatenate(split(jnp.concatenate(values, axis=0)), axis=1)
        placed = lax.dot_general(places, pieces, (((0,), (0,)), ((), ())), preferred_element_type=jnp.float32)
        panel_ref[which * depth : (which + 1) * depth, :] = placed.astype(jnp.bfloat16)
    multiply(out_ref, 1 - core, (own0, own1), (other0, other1), panel_ref)


def second_kernel(place_ref, own0, other0, own1, other1, panel_ref, out_ref):
    multiply(out_ref, place_ref[1], (own0, own1), (other0, other1), panel_ref)


def last_kernel(parts_ref, out_ref):
    total = jnp.sum(parts_ref[...].reshape(-1, 8, LANES), axis=0)
    out_ref[:, :LANES] = total[:4]
    out_ref[:, LANES:] = total[4:]


def per_device(hamiltonian, margin, owner, inverse_blocks, pole_index):
    rows_axis = lax.axis_size("x") * lax.axis_size("core")
    cols_axis = lax.axis_size("yl")
    z_axis = lax.axis_size("z")
    share, width = hamiltonian.shape
    block_rows, depth = inverse_blocks.shape[2:]
    senders = rows_axis * cols_axis
    core = lax.axis_index("core")
    row = lax.axis_index("x") * lax.axis_size("core") + core
    place = jnp.stack([row, core, lax.axis_index("z") % 2]).astype(jnp.int32)
    theta = math.pi * (pole_index[0].astype(jnp.float32) + 0.5) / POLES
    energy, damping = pole_radius * jnp.cos(theta), pole_radius * jnp.sin(theta)
    weight_re, weight_im = weight_scale * jnp.cos(theta), weight_scale * jnp.sin(theta)
    shifted_re = weight_re * energy - weight_im * damping
    shifted_im = weight_re * damping + weight_im * energy
    coefs = jnp.stack([-weight_im, -weight_re, shifted_im, shifted_re])
    pieces = lax.axis_size("x")
    factor = jax.ShapeDtypeStruct((block_rows // 2, 2 * depth), jnp.float32)
    packed, *factors = pl.pallas_call(
        lambda *refs: prepare_kernel(rows_axis, cols_axis, pieces, *refs),
        out_shape=(jax.ShapeDtypeStruct((senders * CHUNK, LANES), jnp.float32), factor, factor),
        in_specs=[SMEM, SMEM] + [HBM] * 4,
        out_specs=(VMEM,) * 3,
        scratch_shapes=[
            pltpu.VMEM((share, LANES), jnp.float32),
            pltpu.VMEM((share, LANES), jnp.float32),
            pltpu.VMEM((1, share), jnp.int32),
            pltpu.VMEM((2, block_rows, depth), jnp.float32),
            pltpu.SemaphoreType.DMA((3 + pieces,)),
        ],
        compiler_params=PREPARE,
        name="pack_rows_and_left_factors",
    )(place, coefs, hamiltonian, margin, owner.reshape(1, share), inverse_blocks[0])
    arrived = lax.all_to_all(
        packed.reshape(senders, 1, CHUNK * LANES), ("x", "core", "yl"), split_axis=0, concat_axis=0, tiled=True
    ).reshape(senders * CHUNK, LANES)
    pairs = (
        [(i, i ^ 1) for i in range(z_axis)],
        [(i, (i - 1 if i % 2 == 0 else i + 1) % z_axis) for i in range(z_axis)],
    )
    others = [lax.ppermute(own, "z", pair) for own, pair in zip(factors, pairs)]
    summed = [factors[0], others[0], factors[1], others[1]]
    chunks = jax.ShapeDtypeStruct((block_rows // 2, LANES), jnp.float32)
    sent, panel = pl.pallas_call(
        lambda *refs: first_kernel(senders, *refs),
        out_shape=(chunks, jax.ShapeDtypeStruct((2 * depth, 2 * LANES), jnp.bfloat16)),
        in_specs=[SMEM] + [VMEM] * 5,
        out_specs=(VMEM,) * 2,
        compiler_params=PARAMS,
        name="place_and_multiply",
    )(place, arrived, *summed)
    received = lax.ppermute(sent, "core", [(0, 1), (1, 0)])
    kept = pl.pallas_call(
        second_kernel,
        out_shape=chunks,
        in_specs=[SMEM] + [VMEM] * 5,
        out_specs=VMEM,
        compiler_params=PARAMS,
        cost_estimate=pl.CostEstimate(flops=3 * block_rows * 2 * depth * LANES, bytes_accessed=4 * block_rows * depth, transcendentals=0),
        name="multiply_own",
    )(place, *summed, panel)
    both = (kept + received).reshape(block_rows // 8, 4, LANES)
    parts = lax.all_to_all(both, ("x", "yh", "z"), split_axis=0, concat_axis=0, tiled=True)
    return pl.pallas_call(
        last_kernel,
        out_shape=jax.ShapeDtypeStruct((4, width), jnp.float32),
        in_specs=[VMEM],
        out_specs=VMEM,
        compiler_params=PARAMS,
        name="sum_parts",
    )(parts.reshape(block_rows // 2, LANES))


def solution(mesh):
    fine = Mesh(mesh.devices.reshape(2, 8, 8, 2, 4), ("yh", "z", "x", "core", "yl"))
    in_specs = (
        P(("x", "core", "yl"), None),
        P(("x", "core", "yl"), None),
        P(("x", "core", "yl")),
        P(("yh", "z"), None, "yl", ("x", "core")),
        P(("yh", "z")),
    )
    out_specs = P(("yl", "x", "core", "yh", "z"), None)
    return jax.shard_map(per_device, mesh=fine, in_specs=in_specs, out_specs=out_specs, check_vma=False)
```

```python
import math

import jax
import jax.numpy as jnp
from jax import lax
from jax.experimental import pallas as pl
from jax.experimental.pallas import tpu as pltpu
from jax.sharding import Mesh, PartitionSpec as P

POLES = 64
pole_radius = 1.5
weight_scale = 0.3

LANES = 128
SLOTS = 8
VMEM = pl.BlockSpec(memory_space=pltpu.VMEM)
SMEM = pl.BlockSpec(memory_space=pltpu.SMEM)
PARAMS = pltpu.CompilerParams(vmem_limit_bytes=40 * 1024 * 1024)


def iota(shape, axis):
    return lax.broadcasted_iota(jnp.int32, shape, axis)


def pack_kernel(rows_axis, cols_axis, ham_ref, mar_ref, owner_ref, out_ref):
    share, width = ham_ref.shape
    shift = (4096 // rows_axis).bit_length() - 1
    own_r = jnp.broadcast_to(owner_ref[...].astype(jnp.float32), (share, share))
    own_c = jnp.sum(jnp.where(iota((share, share), 0) == iota((share, share), 1), own_r, 0.0), axis=1, keepdims=True)
    own_c = jnp.broadcast_to(own_c, (share, share)).astype(jnp.int32)
    own_r = own_r.astype(jnp.int32)
    same = (own_r >> shift) == (own_c >> shift)
    first, second = iota((share, share), 0), iota((share, share), 1)
    rank_r = jnp.sum(jnp.where(same & (first < second), 1.0, 0.0), axis=0, keepdims=True)
    rank_c = jnp.sum(jnp.where(same & (second < first), 1.0, 0.0), axis=1, keepdims=True)
    slot_r = (own_r[:1] >> shift) * SLOTS + rank_r.astype(jnp.int32)
    slot_c = (own_c[:, :1] >> shift) * SLOTS + rank_c.astype(jnp.int32)
    total = rows_axis * SLOTS
    packer = jnp.where(iota((total, share), 0) == jnp.broadcast_to(slot_r, (total, share)), 1.0, 0.0)
    within = (own_c[:, :1] & ((1 << shift) - 1)) + 1
    labels = jnp.where(
        iota((share, total), 1) == jnp.broadcast_to(slot_c, (share, total)),
        jnp.broadcast_to(within, (share, total)).astype(jnp.float32),
        0.0,
    )
    labels = jnp.sum(labels, axis=0, keepdims=True)
    chunk = 2 * width // LANES * SLOTS + 1
    for which, ref in enumerate((ham_ref, mar_ref)):
        packed = jnp.dot(packer, ref[...], precision=lax.Precision.HIGHEST, preferred_element_type=jnp.float32)
        for part in range(width // LANES):
            offset = (which * (width // LANES) + part) * SLOTS
            for row in range(rows_axis):
                tile = packed[row * SLOTS : (row + 1) * SLOTS, part * LANES : (part + 1) * LANES]
                for col in range(cols_axis):
                    base = (row * cols_axis + col) * chunk + offset
                    out_ref[base : base + SLOTS, :] = tile
    for target in range(rows_axis * cols_axis):
        base = (target + 1) * chunk - 1
        out_ref[base : base + 1, :] = labels


def split(value):
    high = value.astype(jnp.bfloat16)
    return high, (value - high.astype(jnp.float32)).astype(jnp.bfloat16)


def left_kernel(place_ref, coef_ref, blocks_ref, *out_refs):
    rows, depth = blocks_ref.shape[1:]
    piece = rows // 16
    odd_here = place_ref[2] == 1
    for index in range(16):
        x, core = divmod(index, 2)
        re = blocks_ref[0, index * piece : (index + 1) * piece, :]
        im = blocks_ref[1, index * piece : (index + 1) * piece, :]
        for which in range(2):
            value = (coef_ref[2 * which] * re + coef_ref[2 * which + 1] * im).reshape(piece // 16, 2, 8, depth)
            first, second = value[:, 0], value[:, 1]
            upper = iota(first.shape, 1) < 4
            even = jnp.where(upper, first, pltpu.roll(second, 4, 1)).reshape(piece // 2, depth)
            odd = jnp.where(upper, pltpu.roll(first, 4, 1), second).reshape(piece // 2, depth)
            at = (slice(x * piece // 2, (x + 1) * piece // 2), slice(which * depth, (which + 1) * depth))
            out_refs[core][at] = jnp.where(odd_here, odd, even)
            out_refs[2 + core][at] = jnp.where(odd_here, even, odd)


def pair_kernel(own_ref, other_ref, high_ref, low_ref):
    high_ref[...], low_ref[...] = split(own_ref[...] + other_ref[...])


def store_chunks(out_ref, value):
    pairs = value.shape[0] // 8
    left = value[:, :LANES].reshape(pairs, 8, LANES)
    right = value[:, LANES:].reshape(pairs, 8, LANES)
    upper = iota((pairs, 8, LANES), 1) < 4
    out_ref[:, 0] = jnp.where(upper, left, pltpu.roll(right, 4, 1))
    out_ref[:, 1] = jnp.where(upper, pltpu.roll(left, 4, 1), right)


def multiply(out_ref, which, highs, lows, panel_high_ref, panel_low_ref):
    dot = lambda a, b: jnp.dot(a, b, preferred_element_type=jnp.float32)
    for index in range(2):

        @pl.when(which == index)
        def _():
            high, low, panel = highs[index][...], lows[index][...], panel_high_ref[...]
            store_chunks(out_ref, dot(high, panel) + (dot(low, panel) + dot(high, panel_low_ref[...])))


def first_kernel(senders, place_ref, rows_ref, high0, low0, high1, low1, out_ref, panel_high_ref, panel_low_ref):
    row, core = place_ref[0], place_ref[1]
    chunk = rows_ref.shape[0] // senders
    depth = panel_high_ref.shape[0] // 2
    parts = (chunk - 1) // SLOTS
    labels = rows_ref[pl.ds(chunk - 1, senders, stride=chunk), :]
    lane = iota((senders, LANES), 1)
    wanted = (iota((senders, depth), 1) + 1).astype(jnp.float32)
    places = []
    for slot in range(SLOTS):
        label = jnp.sum(jnp.where(lane == row * SLOTS + slot, labels, 0.0), axis=1, keepdims=True)
        places.append(jnp.where(jnp.broadcast_to(label, (senders, depth)) == wanted, 1.0, 0.0))
    places = jnp.concatenate(places, axis=0).astype(jnp.bfloat16)
    for part in range(parts):
        values = [rows_ref[pl.ds(part * SLOTS + slot, senders, stride=chunk), :] for slot in range(SLOTS)]
        pieces = split(jnp.concatenate(values, axis=0))
        which, left = divmod(part, parts // 2)
        at = (slice(which * depth, (which + 1) * depth), slice(left * LANES, (left + 1) * LANES))
        for ref, piece in zip((panel_high_ref, panel_low_ref), pieces):
            placed = lax.dot_general(places, piece, (((0,), (0,)), ((), ())), preferred_element_type=jnp.float32)
            ref[at] = placed.astype(jnp.bfloat16)
    multiply(out_ref, 1 - core, (high0, high1), (low0, low1), panel_high_ref, panel_low_ref)


def second_kernel(place_ref, high0, low0, high1, low1, panel_high_ref, panel_low_ref, out_ref):
    multiply(out_ref, place_ref[1], (high0, high1), (low0, low1), panel_high_ref, panel_low_ref)


def last_kernel(parts_ref, out_ref):
    total = jnp.sum(parts_ref[...], axis=0)
    out_ref[:, :LANES] = total[:4]
    out_ref[:, LANES:] = total[4:]


def per_device(hamiltonian, margin, owner, inverse_blocks, pole_index):
    rows_axis = lax.axis_size("x") * lax.axis_size("core")
    cols_axis = lax.axis_size("yl")
    share, width = hamiltonian.shape
    senders = rows_axis * cols_axis
    chunk = 2 * width // LANES * SLOTS + 1
    packed = pl.pallas_call(
        lambda *refs: pack_kernel(rows_axis, cols_axis, *refs),
        out_shape=jax.ShapeDtypeStruct((senders * chunk, LANES), jnp.float32),
        in_specs=[VMEM] * 3,
        out_specs=VMEM,
        compiler_params=PARAMS,
        name="pack_rows",
    )(hamiltonian, margin, owner.reshape(1, share))
    arrived = lax.all_to_all(
        packed.reshape(senders, 1, chunk * LANES), ("x", "core", "yl"), split_axis=0, concat_axis=0, tiled=True
    ).reshape(senders * chunk, LANES)

    theta = math.pi * (pole_index[0].astype(jnp.float32) + 0.5) / POLES
    energy, damping = pole_radius * jnp.cos(theta), pole_radius * jnp.sin(theta)
    weight_re, weight_im = weight_scale * jnp.cos(theta), weight_scale * jnp.sin(theta)
    shifted_re = weight_re * energy - weight_im * damping
    shifted_im = weight_re * damping + weight_im * energy
    coefs = jnp.stack([-weight_im, -weight_re, shifted_im, shifted_re])
    block_rows, depth = inverse_blocks.shape[2:]
    core = lax.axis_index("core")
    place = jnp.stack(
        [lax.axis_index("x") * lax.axis_size("core") + core, core, lax.axis_index("zp")]
    ).astype(jnp.int32)
    factor = jax.ShapeDtypeStruct((block_rows // 4, 2 * depth), jnp.float32)
    factors = pl.pallas_call(
        left_kernel,
        out_shape=(factor,) * 4,
        in_specs=[SMEM, SMEM, VMEM],
        out_specs=(VMEM,) * 4,
        compiler_params=PARAMS,
        cost_estimate=pl.CostEstimate(flops=4 * block_rows * depth, bytes_accessed=16 * block_rows * depth, transcendentals=0),
        name="left_factors",
    )(place, coefs, inverse_blocks[0])
    z_axis = lax.axis_size("zq") * lax.axis_size("zp")
    pairs = (
        [(i, i ^ 1) for i in range(z_axis)],
        [(i, (i - 1 if i % 2 == 0 else i + 1) % z_axis) for i in range(z_axis)],
    )
    part = jax.ShapeDtypeStruct(factor.shape, jnp.bfloat16)
    summed = []
    for own, sent, pair in zip(factors[:2], factors[2:], pairs):
        summed += pl.pallas_call(
            pair_kernel,
            out_shape=(part, part),
            in_specs=[VMEM] * 2,
            out_specs=(VMEM, VMEM),
            compiler_params=PARAMS,
            cost_estimate=pl.CostEstimate(flops=block_rows * depth, bytes_accessed=6 * block_rows * depth, transcendentals=0),
            name="pair_sums",
        )(own, lax.ppermute(sent, ("zq", "zp"), pair))
    chunks = jax.ShapeDtypeStruct((block_rows // 32, 2, 8, LANES), jnp.float32)
    panel = jax.ShapeDtypeStruct((2 * depth, width), jnp.bfloat16)
    sent, panel_high, panel_low = pl.pallas_call(
        lambda *refs: first_kernel(senders, *refs),
        out_shape=(chunks, panel, panel),
        in_specs=[SMEM] + [VMEM] * 5,
        out_specs=(VMEM,) * 3,
        compiler_params=PARAMS,
        name="place_and_multiply",
    )(place, arrived, *summed)
    received = lax.ppermute(sent, "core", [(0, 1), (1, 0)])
    kept = pl.pallas_call(
        second_kernel,
        out_shape=chunks,
        in_specs=[SMEM] + [VMEM] * 6,
        out_specs=VMEM,
        compiler_params=PARAMS,
        cost_estimate=pl.CostEstimate(flops=3 * block_rows * depth * width, bytes_accessed=block_rows * depth * 4, transcendentals=0),
        name="multiply_own",
    )(place, *summed, panel_high, panel_low)
    both = (kept + received).reshape(block_rows // 16, 8, LANES)
    parts = lax.all_to_all(both, ("x", "yh", "zq"), split_axis=0, concat_axis=0, tiled=True)
    return pl.pallas_call(
        last_kernel,
        out_shape=jax.ShapeDtypeStruct((4, width), jnp.float32),
        in_specs=[VMEM],
        out_specs=VMEM,
        compiler_params=PARAMS,
        name="sum_parts",
    )(parts)


def solution(mesh):
    fine = Mesh(mesh.devices.reshape(2, 4, 2, 8, 2, 4), ("yh", "zq", "zp", "x", "core", "yl"))
    in_specs = (
        P(("x", "core", "yl"), None),
        P(("x", "core", "yl"), None),
        P(("x", "core", "yl")),
        P(("yh", "zq", "zp"), None, "yl", ("x", "core")),
        P(("yh", "zq", "zp")),
    )
    out_specs = P(("yl", "x", "core", "yh", "zq", "zp"), None)
    return jax.shard_map(per_device, mesh=fine, in_specs=in_specs, out_specs=out_specs, check_vma=False)
```

```python
import math

import jax
import jax.numpy as jnp
from jax import lax
from jax.experimental import pallas as pl
from jax.experimental.pallas import tpu as pltpu
from jax.sharding import Mesh, PartitionSpec as P

POLES = 64
pole_radius = 1.5
weight_scale = 0.3

LANES = 128
SLOTS = 8
CHUNK = 2 * SLOTS + 1
VMEM = pl.BlockSpec(memory_space=pltpu.VMEM)
SMEM = pl.BlockSpec(memory_space=pltpu.SMEM)
ANY = pl.BlockSpec(memory_space=pl.ANY)
INPUTS = pltpu.CompilerParams(vmem_limit_bytes=56 * 1024 * 1024)
PAIR = pltpu.CompilerParams(vmem_limit_bytes=51 * 1024 * 1024)
PARAMS = pltpu.CompilerParams(vmem_limit_bytes=40 * 1024 * 1024)
PAIR_FLOPS = 5 * 10**9


def iota(shape, axis):
    return lax.broadcasted_iota(jnp.int32, shape, axis)


def pack_kernel(rows_axis, cols_axis, shift, place_ref, ham_ref, mar_ref, owner_ref, out_ref, ham, mar, owner, sems):
    share = ham.shape[0]
    columns = pl.ds(pl.multiple_of(place_ref[2] * LANES, LANES), LANES)
    copies = [
        pltpu.make_async_copy(owner_ref, owner, sems.at[0]),
        pltpu.make_async_copy(ham_ref.at[:, columns], ham, sems.at[1]),
        pltpu.make_async_copy(mar_ref.at[:, columns], mar, sems.at[2]),
    ]
    for copy in copies:
        copy.start()
    copies[0].wait()
    own_r = jnp.broadcast_to(owner[...].astype(jnp.float32), (share, share))
    own_c = jnp.sum(jnp.where(iota((share, share), 0) == iota((share, share), 1), own_r, 0.0), axis=1, keepdims=True)
    own_c = jnp.broadcast_to(own_c, (share, share)).astype(jnp.int32)
    own_r = own_r.astype(jnp.int32)
    same = (own_r >> shift) == (own_c >> shift)
    first, second = iota((share, share), 0), iota((share, share), 1)
    rank_r = jnp.sum(jnp.where(same & (first < second), 1.0, 0.0), axis=0, keepdims=True)
    rank_c = jnp.sum(jnp.where(same & (second < first), 1.0, 0.0), axis=1, keepdims=True)
    slot_r = (own_r[:1] >> shift) * SLOTS + rank_r.astype(jnp.int32)
    slot_c = (own_c[:, :1] >> shift) * SLOTS + rank_c.astype(jnp.int32)
    total = rows_axis * SLOTS
    packer = jnp.where(iota((total, share), 0) == jnp.broadcast_to(slot_r, (total, share)), 1.0, 0.0)
    within = (own_c[:, :1] & ((1 << shift) - 1)) + 1
    labels = jnp.where(
        iota((share, total), 1) == jnp.broadcast_to(slot_c, (share, total)),
        jnp.broadcast_to(within, (share, total)).astype(jnp.float32),
        0.0,
    )
    labels = jnp.sum(labels, axis=0, keepdims=True)
    for target in range(rows_axis * cols_axis):
        base = (target + 1) * CHUNK - 1
        out_ref[base : base + 1, :] = labels
    for which, ref in enumerate((ham, mar)):
        copies[1 + which].wait()
        packed = jnp.dot(packer, ref[...], precision=lax.Precision.HIGHEST, preferred_element_type=jnp.float32)
        for row in range(rows_axis):
            tile = packed[row * SLOTS : (row + 1) * SLOTS]
            for col in range(cols_axis):
                base = (row * cols_axis + col) * CHUNK + which * SLOTS
                out_ref[base : base + SLOTS, :] = tile


def split(value):
    high = value.astype(jnp.bfloat16)
    return high, (value - high.astype(jnp.float32)).astype(jnp.bfloat16)


def coefficient_kernel(pieces, coef_ref, blocks_ref, first_ref, second_ref, blocks, sems):
    rows, depth = blocks.shape[1:]
    piece = rows // pieces
    half = piece // 2
    copies = []
    for x in range(pieces):
        at = pl.ds(x * piece, piece)
        copies.append(pltpu.make_async_copy(blocks_ref.at[:, at], blocks.at[:, at], sems.at[x]))
        copies[-1].start()
    for x in range(pieces):
        copies[x].wait()
        for core, ref in enumerate((first_ref, second_ref)):
            at = slice(x * piece + core * half, x * piece + (core + 1) * half)
            re, im = blocks[0, at, :], blocks[1, at, :]
            for which in range(2):
                value = coef_ref[2 * which] * re + coef_ref[2 * which + 1] * im
                ref[x * half : (x + 1) * half, which * depth : (which + 1) * depth] = value


def pair_kernel(core, coef_ref, blocks_ref, other_ref, sum_ref, blocks, sems):
    pieces, half, depth = blocks.shape[1:]
    steps = sems.shape[0]
    step = pieces // steps
    copies = []
    for at in range(steps):
        x = pl.ds(at * step, step)
        copies.append(pltpu.make_async_copy(blocks_ref.at[:, x, core], blocks.at[:, x], sems.at[at]))
        copies[-1].start()
    for at in range(steps):
        copies[at].wait()
        for x in range(at * step, (at + 1) * step):
            re, im = blocks[0, x], blocks[1, x]
            rows = slice(x * half, (x + 1) * half)
            for which in range(2):
                columns = slice(which * depth, (which + 1) * depth)
                own = coef_ref[2 * which] * re + coef_ref[2 * which + 1] * im
                sum_ref[rows, columns] = own + other_ref[rows, columns]


def multiply(out_ref, which, sums, panel_ref):
    panel = panel_ref[...]
    for index in range(2):

        @pl.when(which == index)
        def _():
            high, low = split(sums[index][...])
            both = jnp.dot(high, panel, preferred_element_type=jnp.float32)
            more = jnp.dot(low, panel[:, :LANES], preferred_element_type=jnp.float32)
            out_ref[...] = both[:, :LANES] + (both[:, LANES:] + more)


def first_kernel(senders, place_ref, rows_ref, sum0, sum1, out_ref, panel_ref):
    row, core = place_ref[0], place_ref[1]
    depth = panel_ref.shape[0] // 2
    labels = rows_ref[pl.ds(CHUNK - 1, senders, stride=CHUNK), :]
    lane = iota((senders, LANES), 1)
    wanted = (iota((senders, depth), 1) + 1).astype(jnp.float32)
    places = []
    for slot in range(SLOTS):
        label = jnp.sum(jnp.where(lane == row * SLOTS + slot, labels, 0.0), axis=1, keepdims=True)
        places.append(jnp.where(jnp.broadcast_to(label, (senders, depth)) == wanted, 1.0, 0.0))
    places = jnp.concatenate(places, axis=0).astype(jnp.bfloat16)
    for which in range(2):
        values = [rows_ref[pl.ds(which * SLOTS + slot, senders, stride=CHUNK), :] for slot in range(SLOTS)]
        pieces = jnp.concatenate(split(jnp.concatenate(values, axis=0)), axis=1)
        placed = lax.dot_general(places, pieces, (((0,), (0,)), ((), ())), preferred_element_type=jnp.float32)
        panel_ref[which * depth : (which + 1) * depth, :] = placed.astype(jnp.bfloat16)
    multiply(out_ref, 1 - core, (sum0, sum1), panel_ref)


def second_kernel(place_ref, sum0, sum1, panel_ref, out_ref):
    multiply(out_ref, place_ref[1], (sum0, sum1), panel_ref)


def last_kernel(parts_ref, out_ref):
    total = jnp.sum(parts_ref[...].reshape(-1, 8, LANES), axis=0)
    out_ref[:, :LANES] = total[:4]
    out_ref[:, LANES:] = total[4:]


def per_device(hamiltonian, margin, owner, inverse_blocks, pole_index):
    rows_axis = lax.axis_size("x") * lax.axis_size("core")
    cols_axis = lax.axis_size("yl")
    z_axis = lax.axis_size("z")
    share, width = hamiltonian.shape
    block_rows, depth = inverse_blocks.shape[2:]
    senders = rows_axis * cols_axis
    core = lax.axis_index("core")
    row = lax.axis_index("x") * lax.axis_size("core") + core
    place = jnp.stack([row, core, lax.axis_index("z") % 2]).astype(jnp.int32)
    packed = pl.pallas_call(
        lambda *refs: pack_kernel(rows_axis, cols_axis, depth.bit_length() - 1, *refs),
        out_shape=jax.ShapeDtypeStruct((senders * CHUNK, LANES), jnp.float32),
        in_specs=[SMEM, ANY, ANY, ANY],
        out_specs=VMEM,
        scratch_shapes=[
            pltpu.VMEM((share, LANES), jnp.float32),
            pltpu.VMEM((share, LANES), jnp.float32),
            pltpu.VMEM((1, share), jnp.int32),
            pltpu.SemaphoreType.DMA((3,)),
        ],
        compiler_params=INPUTS,
        name="pack_rows",
    )(place, hamiltonian, margin, owner.reshape(1, share))
    arrived = lax.all_to_all(
        packed.reshape(senders, 1, CHUNK * LANES), ("x", "core", "yl"), split_axis=0, concat_axis=0, tiled=True
    ).reshape(senders * CHUNK, LANES)

    theta = math.pi * (pole_index[0].astype(jnp.float32) + 0.5) / POLES
    energy, damping = pole_radius * jnp.cos(theta), pole_radius * jnp.sin(theta)
    weight_re, weight_im = weight_scale * jnp.cos(theta), weight_scale * jnp.sin(theta)
    shifted_re = weight_re * energy - weight_im * damping
    shifted_im = weight_re * damping + weight_im * energy
    coefs = jnp.stack([-weight_im, -weight_re, shifted_im, shifted_re])
    pieces = lax.axis_size("x")
    factor = jax.ShapeDtypeStruct((block_rows // 2, 2 * depth), jnp.float32)
    factors = pl.pallas_call(
        lambda *refs: coefficient_kernel(pieces, *refs),
        out_shape=(factor, factor),
        in_specs=[SMEM, ANY],
        out_specs=(VMEM, VMEM),
        scratch_shapes=[pltpu.VMEM((2, block_rows, depth), jnp.float32), pltpu.SemaphoreType.DMA((pieces,))],
        compiler_params=INPUTS,
        cost_estimate=pl.CostEstimate(flops=6 * block_rows * depth, bytes_accessed=16 * block_rows * depth, transcendentals=0),
        name="left_factors",
    )(coefs, inverse_blocks[0])
    pairs = (
        [(i, i ^ 1) for i in range(z_axis)],
        [(i, (i - 1 if i % 2 == 0 else i + 1) % z_axis) for i in range(z_axis)],
    )
    others = [lax.ppermute(own, "z", pair) for own, pair in zip(factors, pairs)]
    split_blocks = inverse_blocks[0].reshape(2, pieces, 2, block_rows // pieces // 2, depth)
    summed = []
    for which, other in enumerate(others):
        summed.append(
            pl.pallas_call(
                lambda *refs, which=which: pair_kernel(which, *refs),
                out_shape=factor,
                in_specs=[SMEM, ANY, VMEM],
                out_specs=VMEM,
                scratch_shapes=[
                    pltpu.VMEM((2, pieces, block_rows // pieces // 2, depth), jnp.float32),
                    pltpu.SemaphoreType.DMA((4,)),
                ],
                input_output_aliases={2: 0},
                compiler_params=PAIR,
                cost_estimate=pl.CostEstimate(flops=PAIR_FLOPS, bytes_accessed=12 * block_rows * depth, transcendentals=0),
                name="pair_sums",
            )(coefs, split_blocks, other)
        )

    chunks = jax.ShapeDtypeStruct((block_rows // 2, LANES), jnp.float32)
    sent, panel = pl.pallas_call(
        lambda *refs: first_kernel(senders, *refs),
        out_shape=(chunks, jax.ShapeDtypeStruct((2 * depth, 2 * LANES), jnp.bfloat16)),
        in_specs=[SMEM] + [VMEM] * 3,
        out_specs=(VMEM,) * 2,
        compiler_params=PARAMS,
        name="place_and_multiply",
    )(place, arrived, *summed)
    received = lax.ppermute(sent, "core", [(0, 1), (1, 0)])
    kept = pl.pallas_call(
        second_kernel,
        out_shape=chunks,
        in_specs=[SMEM] + [VMEM] * 3,
        out_specs=VMEM,
        compiler_params=PARAMS,
        cost_estimate=pl.CostEstimate(flops=3 * block_rows * 2 * depth * LANES, bytes_accessed=4 * block_rows * depth, transcendentals=0),
        name="multiply_own",
    )(place, *summed, panel)
    both = (kept + received).reshape(block_rows // 8, 4, LANES)
    parts = lax.all_to_all(both, ("x", "yh", "z"), split_axis=0, concat_axis=0, tiled=True)
    return pl.pallas_call(
        last_kernel,
        out_shape=jax.ShapeDtypeStruct((4, width), jnp.float32),
        in_specs=[VMEM],
        out_specs=VMEM,
        compiler_params=PARAMS,
        name="sum_parts",
    )(parts.reshape(block_rows // 2, LANES))


def solution(mesh):
    fine = Mesh(mesh.devices.reshape(2, 8, 8, 2, 4), ("yh", "z", "x", "core", "yl"))
    in_specs = (
        P(("x", "core", "yl"), None),
        P(("x", "core", "yl"), None),
        P(("x", "core", "yl")),
        P(("yh", "z"), None, "yl", ("x", "core")),
        P(("yh", "z")),
    )
    out_specs = P(("yl", "x", "core", "yh", "z"), None)
    return jax.shard_map(per_device, mesh=fine, in_specs=in_specs, out_specs=out_specs, check_vma=False)
```

```python
import math

import jax
import jax.numpy as jnp
from jax import lax
from jax.experimental import pallas as pl
from jax.experimental.pallas import tpu as pltpu
from jax.sharding import Mesh, PartitionSpec as P

POLES = 64
pole_radius = 1.5
weight_scale = 0.3

LANES = 128
SLOTS = 8
VMEM = pl.BlockSpec(memory_space=pltpu.VMEM)
SMEM = pl.BlockSpec(memory_space=pltpu.SMEM)
ANY = pl.BlockSpec(memory_space=pl.ANY)
INPUTS = pltpu.CompilerParams(vmem_limit_bytes=56 * 1024 * 1024)
PARAMS = pltpu.CompilerParams(vmem_limit_bytes=40 * 1024 * 1024)


def iota(shape, axis):
    return lax.broadcasted_iota(jnp.int32, shape, axis)


def pack_kernel(rows_axis, cols_axis, *refs):
    ham, mar, owner, sems = refs[4:]
    out_ref = refs[3]
    share, width = ham.shape
    shift = (share * cols_axis).bit_length() - 1
    copies = [pltpu.make_async_copy(ref, to, sems.at[i]) for i, (ref, to) in enumerate(zip(refs[:3], (ham, mar, owner)))]
    for copy in reversed(copies):
        copy.start()
    copies[2].wait()
    own_r = jnp.broadcast_to(owner[...].astype(jnp.float32), (share, share))
    own_c = jnp.sum(jnp.where(iota((share, share), 0) == iota((share, share), 1), own_r, 0.0), axis=1, keepdims=True)
    own_c = jnp.broadcast_to(own_c, (share, share)).astype(jnp.int32)
    own_r = own_r.astype(jnp.int32)
    same = (own_r >> shift) == (own_c >> shift)
    first, second = iota((share, share), 0), iota((share, share), 1)
    rank_r = jnp.sum(jnp.where(same & (first < second), 1.0, 0.0), axis=0, keepdims=True)
    rank_c = jnp.sum(jnp.where(same & (second < first), 1.0, 0.0), axis=1, keepdims=True)
    slot_r = (own_r[:1] >> shift) * SLOTS + rank_r.astype(jnp.int32)
    slot_c = (own_c[:, :1] >> shift) * SLOTS + rank_c.astype(jnp.int32)
    total = rows_axis * SLOTS
    packer = jnp.where(iota((total, share), 0) == jnp.broadcast_to(slot_r, (total, share)), 1.0, 0.0)
    within = (own_c[:, :1] & ((1 << shift) - 1)) + 1
    labels = jnp.where(
        iota((share, total), 1) == jnp.broadcast_to(slot_c, (share, total)),
        jnp.broadcast_to(within, (share, total)).astype(jnp.float32),
        0.0,
    )
    labels = jnp.sum(labels, axis=0, keepdims=True)
    chunk = 2 * width // LANES * SLOTS + 1
    for target in range(rows_axis * cols_axis):
        base = (target + 1) * chunk - 1
        out_ref[base : base + 1, :] = labels
    for which, ref in enumerate((ham, mar)):
        copies[which].wait()
        packed = jnp.dot(packer, ref[...], precision=lax.Precision.HIGHEST, preferred_element_type=jnp.float32)
        for part in range(width // LANES):
            offset = (which * (width // LANES) + part) * SLOTS
            for row in range(rows_axis):
                tile = packed[row * SLOTS : (row + 1) * SLOTS, part * LANES : (part + 1) * LANES]
                for col in range(cols_axis):
                    base = (row * cols_axis + col) * chunk + offset
                    out_ref[base : base + SLOTS, :] = tile


def split(value):
    high = value.astype(jnp.bfloat16)
    return high, (value - high.astype(jnp.float32)).astype(jnp.bfloat16)


def left_kernel(place_ref, coef_ref, blocks_ref, *out_refs):
    rows, depth = blocks_ref.shape[1:]
    piece = rows // 16
    odd_here = place_ref[2] == 1
    for index in range(16):
        x, core = divmod(index, 2)
        re = blocks_ref[0, index * piece : (index + 1) * piece, :]
        im = blocks_ref[1, index * piece : (index + 1) * piece, :]
        for which in range(2):
            value = coef_ref[2 * which] * re + coef_ref[2 * which + 1] * im
            value = value.reshape(2, 2, 2, 8, depth)
            first, second = value[:, 0], value[:, 1]
            upper = iota(first.shape, 2) < 4
            even = jnp.where(upper, first, pltpu.roll(second, 4, 2))
            odd = jnp.where(upper, pltpu.roll(first, 4, 2), second)
            here = jnp.where(odd_here, odd, even)
            there = jnp.where(odd_here, even, odd)
            columns = slice(which * depth, (which + 1) * depth)
            for part in range(2):
                start = part * rows // 8 + x * piece // 4
                at = (slice(start, start + piece // 4), columns)
                out_refs[core][at] = here[:, part].reshape(piece // 4, depth)
                out_refs[2 + core][at] = there[:, part].reshape(piece // 4, depth)


def first_pair_kernel(place_ref, own_ref, other_ref, here_ref, there_ref):
    rows = here_ref.shape[0]
    half = place_ref[3]
    for ref, which in ((here_ref, half), (there_ref, 1 - half)):
        at = pl.ds(pl.multiple_of(which * rows, rows), rows)
        ref[...] = own_ref[at, :] + other_ref[at, :]


def pair_kernel(own_ref, other_ref, high_ref, low_ref):
    high_ref[...], low_ref[...] = split(own_ref[...] + other_ref[...])


def store_chunks(out_ref, value):
    pairs = value.shape[0] // 8
    left = value[:, :LANES].reshape(pairs, 8, LANES)
    right = value[:, LANES:].reshape(pairs, 8, LANES)
    upper = iota((pairs, 8, LANES), 1) < 4
    out_ref[:, 0] = jnp.where(upper, left, pltpu.roll(right, 4, 1))
    out_ref[:, 1] = jnp.where(upper, pltpu.roll(left, 4, 1), right)


def multiply(out_ref, which, highs, lows, panel_high_ref, panel_low_ref):
    dot = lambda a, b: jnp.dot(a, b, preferred_element_type=jnp.float32)
    for index in range(2):

        @pl.when(which == index)
        def _():
            high, low, panel = highs[index][...], lows[index][...], panel_high_ref[...]
            store_chunks(out_ref, dot(high, panel) + (dot(low, panel) + dot(high, panel_low_ref[...])))


def first_kernel(senders, place_ref, rows_ref, high0, low0, high1, low1, out_ref, panel_high_ref, panel_low_ref):
    row, core = place_ref[0], place_ref[1]
    chunk = rows_ref.shape[0] // senders
    depth = panel_high_ref.shape[0] // 2
    parts = (chunk - 1) // SLOTS
    labels = rows_ref[pl.ds(chunk - 1, senders, stride=chunk), :]
    lane = iota((senders, LANES), 1)
    wanted = (iota((senders, depth), 1) + 1).astype(jnp.float32)
    places = []
    for slot in range(SLOTS):
        label = jnp.sum(jnp.where(lane == row * SLOTS + slot, labels, 0.0), axis=1, keepdims=True)
        places.append(jnp.where(jnp.broadcast_to(label, (senders, depth)) == wanted, 1.0, 0.0))
    places = jnp.concatenate(places, axis=0).astype(jnp.bfloat16)
    for part in range(parts):
        values = [rows_ref[pl.ds(part * SLOTS + slot, senders, stride=chunk), :] for slot in range(SLOTS)]
        pieces = split(jnp.concatenate(values, axis=0))
        which, left = divmod(part, parts // 2)
        at = (slice(which * depth, (which + 1) * depth), slice(left * LANES, (left + 1) * LANES))
        for ref, piece in zip((panel_high_ref, panel_low_ref), pieces):
            placed = lax.dot_general(places, piece, (((0,), (0,)), ((), ())), preferred_element_type=jnp.float32)
            ref[at] = placed.astype(jnp.bfloat16)
    multiply(out_ref, 1 - core, (high0, high1), (low0, low1), panel_high_ref, panel_low_ref)


def second_kernel(place_ref, high0, low0, high1, low1, panel_high_ref, panel_low_ref, out_ref):
    multiply(out_ref, place_ref[1], (high0, high1), (low0, low1), panel_high_ref, panel_low_ref)


def last_kernel(parts_ref, out_ref):
    total = jnp.sum(parts_ref[...], axis=0)
    out_ref[:, :LANES] = total[:4]
    out_ref[:, LANES:] = total[4:]


def per_device(hamiltonian, margin, owner, inverse_blocks, pole_index):
    rows_axis = lax.axis_size("x") * lax.axis_size("core")
    cols_axis = lax.axis_size("yl")
    share, width = hamiltonian.shape
    senders = rows_axis * cols_axis
    chunk = 2 * width // LANES * SLOTS + 1
    packed = pl.pallas_call(
        lambda *refs: pack_kernel(rows_axis, cols_axis, *refs),
        out_shape=jax.ShapeDtypeStruct((senders * chunk, LANES), jnp.float32),
        in_specs=[ANY] * 3,
        out_specs=VMEM,
        scratch_shapes=[
            pltpu.VMEM((share, width), jnp.float32),
            pltpu.VMEM((share, width), jnp.float32),
            pltpu.VMEM((1, share), jnp.int32),
            pltpu.SemaphoreType.DMA((3,)),
        ],
        compiler_params=INPUTS,
        name="pack_rows",
    )(hamiltonian, margin, owner.reshape(1, share))
    arrived = lax.all_to_all(
        packed.reshape(senders, 1, chunk * LANES), ("x", "core", "yl"), split_axis=0, concat_axis=0, tiled=True
    ).reshape(senders * chunk, LANES)

    theta = math.pi * (pole_index[0].astype(jnp.float32) + 0.5) / POLES
    energy, damping = pole_radius * jnp.cos(theta), pole_radius * jnp.sin(theta)
    weight_re, weight_im = weight_scale * jnp.cos(theta), weight_scale * jnp.sin(theta)
    shifted_re = weight_re * energy - weight_im * damping
    shifted_im = weight_re * damping + weight_im * energy
    coefs = jnp.stack([-weight_im, -weight_re, shifted_im, shifted_re])
    block_rows, depth = inverse_blocks.shape[2:]
    core = lax.axis_index("core")
    place = jnp.stack(
        [lax.axis_index("x") * lax.axis_size("core") + core, core, lax.axis_index("zp"), lax.axis_index("zqp")]
    ).astype(jnp.int32)
    factor = jax.ShapeDtypeStruct((block_rows // 4, 2 * depth), jnp.float32)
    factors = pl.pallas_call(
        left_kernel,
        out_shape=(factor,) * 4,
        in_specs=[SMEM, SMEM, VMEM],
        out_specs=(VMEM,) * 4,
        compiler_params=PARAMS,
        cost_estimate=pl.CostEstimate(flops=4 * block_rows * depth, bytes_accessed=16 * block_rows * depth, transcendentals=0),
        name="left_factors",
    )(place, coefs, inverse_blocks[0])
    def pairings(size):
        return (
            [(i, i ^ 1) for i in range(size)],
            [(i, (i - 1 if i % 2 == 0 else i + 1) % size) for i in range(size)],
        )

    quarter = jax.ShapeDtypeStruct((block_rows // 8, 2 * depth), jnp.float32)
    part = jax.ShapeDtypeStruct(quarter.shape, jnp.bfloat16)
    seconds = []
    for own, sent, pair in zip(factors[:2], factors[2:], pairings(8)):
        seconds.append(
            pl.pallas_call(
                first_pair_kernel,
                out_shape=(quarter, quarter),
                in_specs=[SMEM, VMEM, VMEM],
                out_specs=(VMEM, VMEM),
                compiler_params=PARAMS,
                cost_estimate=pl.CostEstimate(flops=block_rows * depth // 2, bytes_accessed=6 * block_rows * depth, transcendentals=0),
                name="first_pair_sums",
            )(place, own, lax.ppermute(sent, ("zqq", "zqp", "zp"), pair))
        )
    summed = []
    for (own, sent), pair in zip(seconds, pairings(4)):
        summed += pl.pallas_call(
            pair_kernel,
            out_shape=(part, part),
            in_specs=[VMEM] * 2,
            out_specs=(VMEM, VMEM),
            compiler_params=PARAMS,
            cost_estimate=pl.CostEstimate(flops=block_rows * depth // 2, bytes_accessed=3 * block_rows * depth, transcendentals=0),
            name="second_pair_sums",
        )(own, lax.ppermute(sent, ("zqq", "zqp"), pair))
    chunks = jax.ShapeDtypeStruct((block_rows // 64, 2, 8, LANES), jnp.float32)
    panel = jax.ShapeDtypeStruct((2 * depth, width), jnp.bfloat16)
    sent, panel_high, panel_low = pl.pallas_call(
        lambda *refs: first_kernel(senders, *refs),
        out_shape=(chunks, panel, panel),
        in_specs=[SMEM] + [VMEM] * 5,
        out_specs=(VMEM,) * 3,
        compiler_params=PARAMS,
        name="place_and_multiply",
    )(place, arrived, *summed)
    received = lax.ppermute(sent, "core", [(0, 1), (1, 0)])
    kept = pl.pallas_call(
        second_kernel,
        out_shape=chunks,
        in_specs=[SMEM] + [VMEM] * 6,
        out_specs=VMEM,
        compiler_params=PARAMS,
        cost_estimate=pl.CostEstimate(flops=3 * block_rows * depth * width, bytes_accessed=block_rows * depth * 4, transcendentals=0),
        name="multiply_own",
    )(place, *summed, panel_high, panel_low)
    both = (kept + received).reshape(block_rows // 32, 8, LANES)
    parts = lax.all_to_all(both, ("x", "yh", "zqq"), split_axis=0, concat_axis=0, tiled=True)
    return pl.pallas_call(
        last_kernel,
        out_shape=jax.ShapeDtypeStruct((4, width), jnp.float32),
        in_specs=[VMEM],
        out_specs=VMEM,
        compiler_params=PARAMS,
        name="sum_parts",
    )(parts)


def solution(mesh):
    fine = Mesh(mesh.devices.reshape(2, 2, 2, 2, 8, 2, 4), ("yh", "zqq", "zqp", "zp", "x", "core", "yl"))
    in_specs = (
        P(("x", "core", "yl"), None),
        P(("x", "core", "yl"), None),
        P(("x", "core", "yl")),
        P(("yh", "zqq", "zqp", "zp"), None, "yl", ("x", "core")),
        P(("yh", "zqq", "zqp", "zp")),
    )
    out_specs = P(("yl", "x", "core", "yh", "zqq", "zqp", "zp"), None)
    return jax.shard_map(per_device, mesh=fine, in_specs=in_specs, out_specs=out_specs, check_vma=False)
```

```python
import math

import jax
import jax.numpy as jnp
from jax import lax
from jax.experimental import pallas as pl
from jax.experimental.pallas import tpu as pltpu
from jax.sharding import Mesh, PartitionSpec as P

POLES = 64
pole_radius = 1.5
weight_scale = 0.3

LANES = 128
SLOTS = 8
VMEM = pl.BlockSpec(memory_space=pltpu.VMEM)
SMEM = pl.BlockSpec(memory_space=pltpu.SMEM)
ANY = pl.BlockSpec(memory_space=pl.ANY)
INPUTS = pltpu.CompilerParams(vmem_limit_bytes=56 * 1024 * 1024)
PARAMS = pltpu.CompilerParams(vmem_limit_bytes=40 * 1024 * 1024)


def iota(shape, axis):
    return lax.broadcasted_iota(jnp.int32, shape, axis)


def pack_kernel(rows_axis, cols_axis, *refs):
    ham, mar, owner, sems = refs[4:]
    out_ref = refs[3]
    share, width = ham.shape
    shift = (share * cols_axis).bit_length() - 1
    copies = [pltpu.make_async_copy(ref, to, sems.at[i]) for i, (ref, to) in enumerate(zip(refs[:3], (ham, mar, owner)))]
    for copy in reversed(copies):
        copy.start()
    copies[2].wait()
    own_r = jnp.broadcast_to(owner[...].astype(jnp.float32), (share, share))
    own_c = jnp.sum(jnp.where(iota((share, share), 0) == iota((share, share), 1), own_r, 0.0), axis=1, keepdims=True)
    own_c = jnp.broadcast_to(own_c, (share, share)).astype(jnp.int32)
    own_r = own_r.astype(jnp.int32)
    same = (own_r >> shift) == (own_c >> shift)
    first, second = iota((share, share), 0), iota((share, share), 1)
    rank_r = jnp.sum(jnp.where(same & (first < second), 1.0, 0.0), axis=0, keepdims=True)
    rank_c = jnp.sum(jnp.where(same & (second < first), 1.0, 0.0), axis=1, keepdims=True)
    slot_r = (own_r[:1] >> shift) * SLOTS + rank_r.astype(jnp.int32)
    slot_c = (own_c[:, :1] >> shift) * SLOTS + rank_c.astype(jnp.int32)
    total = rows_axis * SLOTS
    packer = jnp.where(iota((total, share), 0) == jnp.broadcast_to(slot_r, (total, share)), 1.0, 0.0)
    within = (own_c[:, :1] & ((1 << shift) - 1)) + 1
    labels = jnp.where(
        iota((share, total), 1) == jnp.broadcast_to(slot_c, (share, total)),
        jnp.broadcast_to(within, (share, total)).astype(jnp.float32),
        0.0,
    )
    labels = jnp.sum(labels, axis=0, keepdims=True)
    chunk = 2 * width // LANES * SLOTS + 1
    for target in range(rows_axis * cols_axis):
        base = (target + 1) * chunk - 1
        out_ref[base : base + 1, :] = labels
    wide = 2 * SLOTS
    for which, ref in enumerate((ham, mar)):
        copies[which].wait()
        packed = jnp.dot(packer, ref[...], precision=lax.Precision.HIGHEST, preferred_element_type=jnp.float32)
        for row in range(rows_axis):
            x, core = divmod(row, 2)
            tile = packed[x * wide : (x + 1) * wide, core * LANES : (core + 1) * LANES]
            for col in range(cols_axis):
                base = (row * cols_axis + col) * chunk + which * wide
                out_ref[base : base + wide, :] = tile


def split(value):
    high = value.astype(jnp.bfloat16)
    return high, (value - high.astype(jnp.float32)).astype(jnp.bfloat16)


def left_kernel(place_ref, coef_ref, blocks_ref, *out_refs):
    rows, depth = blocks_ref.shape[1:]
    piece = rows // 16
    odd_here = place_ref[2] == 1
    for index in range(16):
        x, core = divmod(index, 2)
        re = blocks_ref[0, index * piece : (index + 1) * piece, :]
        im = blocks_ref[1, index * piece : (index + 1) * piece, :]
        for which in range(2):
            value = (coef_ref[2 * which] * re + coef_ref[2 * which + 1] * im).reshape(piece // 16, 2, 8, depth)
            first, second = value[:, 0], value[:, 1]
            upper = iota(first.shape, 1) < 4
            even = jnp.where(upper, first, pltpu.roll(second, 4, 1)).reshape(piece // 2, depth)
            odd = jnp.where(upper, pltpu.roll(first, 4, 1), second).reshape(piece // 2, depth)
            at = (slice(x * piece // 2, (x + 1) * piece // 2), slice(which * depth, (which + 1) * depth))
            out_refs[core][at] = jnp.where(odd_here, odd, even)
            out_refs[2 + core][at] = jnp.where(odd_here, even, odd)


def pair_kernel(own_ref, other_ref, sum_ref):
    sum_ref[...] = own_ref[...] + other_ref[...]


def product_kernel(senders, pieces, place_ref, rows_ref, own0, own1, mate0, mate1, out_ref, panel_ref):
    chunk = rows_ref.shape[0] // senders
    depth = panel_ref.shape[1] // 2
    labels = rows_ref[pl.ds(chunk - 1, senders, stride=chunk), :]
    lane = iota((senders, LANES), 1)
    wanted = (iota((senders, depth), 1) + 1).astype(jnp.float32)
    for block in range(2):
        places = []
        for slot in range(SLOTS):
            at = (2 * place_ref[0] + block) * SLOTS + slot
            label = jnp.sum(jnp.where(lane == at, labels, 0.0), axis=1, keepdims=True)
            places.append(jnp.where(jnp.broadcast_to(label, (senders, depth)) == wanted, 1.0, 0.0))
        places = jnp.concatenate(places, axis=0).astype(jnp.bfloat16)
        for which in range(2):
            start = (2 * which + block) * SLOTS
            values = [rows_ref[pl.ds(start + slot, senders, stride=chunk), :] for slot in range(SLOTS)]
            parts = jnp.concatenate(split(jnp.concatenate(values, axis=0)), axis=1)
            placed = lax.dot_general(places, parts, (((0,), (0,)), ((), ())), preferred_element_type=jnp.float32)
            panel_ref[block, which * depth : (which + 1) * depth, :] = placed.astype(jnp.bfloat16)
    for core in range(2):

        @pl.when(place_ref[1] == core)
        def _():
            for row_core, pair in enumerate(((own0, mate0), (own1, mate1))):
                total = None
                for block in range(2):
                    high, low = split(pair[block ^ core][...])
                    panel = panel_ref[block]
                    both = jnp.dot(high, panel, preferred_element_type=jnp.float32)
                    more = jnp.dot(low, panel[:, :LANES], preferred_element_type=jnp.float32)
                    term = both[:, :LANES] + (both[:, LANES:] + more)
                    total = term if total is None else total + term
                size = total.shape[0] // pieces
                for x in range(pieces):
                    start = (2 * x + row_core) * size
                    out_ref[start : start + size, :] = total[x * size : (x + 1) * size]


def last_kernel(pieces, parts_ref, out_ref):
    parts = parts_ref[...].reshape(pieces, 2, -1, 8, LANES)
    total = jnp.sum(jnp.sum(parts, axis=2), axis=0)
    total = total[:, :4] + total[:, 4:]
    out_ref[:, :LANES] = total[0]
    out_ref[:, LANES:] = total[1]


def per_device(hamiltonian, margin, owner, inverse_blocks, pole_index):
    rows_axis = lax.axis_size("x") * lax.axis_size("core")
    cols_axis = lax.axis_size("yl")
    share, width = hamiltonian.shape
    senders = rows_axis * cols_axis
    chunk = 2 * width // LANES * SLOTS + 1
    packed = pl.pallas_call(
        lambda *refs: pack_kernel(rows_axis, cols_axis, *refs),
        out_shape=jax.ShapeDtypeStruct((senders * chunk, LANES), jnp.float32),
        in_specs=[ANY] * 3,
        out_specs=VMEM,
        scratch_shapes=[
            pltpu.VMEM((share, width), jnp.float32),
            pltpu.VMEM((share, width), jnp.float32),
            pltpu.VMEM((1, share), jnp.int32),
            pltpu.SemaphoreType.DMA((3,)),
        ],
        compiler_params=INPUTS,
        name="pack_rows",
    )(hamiltonian, margin, owner.reshape(1, share))
    arrived = lax.all_to_all(
        packed.reshape(senders, 1, chunk * LANES), ("x", "core", "yl"), split_axis=0, concat_axis=0, tiled=True
    ).reshape(senders * chunk, LANES)

    theta = math.pi * (pole_index[0].astype(jnp.float32) + 0.5) / POLES
    energy, damping = pole_radius * jnp.cos(theta), pole_radius * jnp.sin(theta)
    weight_re, weight_im = weight_scale * jnp.cos(theta), weight_scale * jnp.sin(theta)
    shifted_re = weight_re * energy - weight_im * damping
    shifted_im = weight_re * damping + weight_im * energy
    coefs = jnp.stack([-weight_im, -weight_re, shifted_im, shifted_re])
    block_rows, depth = inverse_blocks.shape[2:]
    core = lax.axis_index("core")
    place = jnp.stack(
        [lax.axis_index("x"), core, lax.axis_index("zp")]
    ).astype(jnp.int32)
    factor = jax.ShapeDtypeStruct((block_rows // 4, 2 * depth), jnp.float32)
    factors = pl.pallas_call(
        left_kernel,
        out_shape=(factor,) * 4,
        in_specs=[SMEM, SMEM, VMEM],
        out_specs=(VMEM,) * 4,
        compiler_params=PARAMS,
        cost_estimate=pl.CostEstimate(flops=4 * block_rows * depth, bytes_accessed=16 * block_rows * depth, transcendentals=0),
        name="left_factors",
    )(place, coefs, inverse_blocks[0])
    z_axis = lax.axis_size("zq") * lax.axis_size("zp")
    pairs = (
        [(i, i ^ 1) for i in range(z_axis)],
        [(i, (i - 1 if i % 2 == 0 else i + 1) % z_axis) for i in range(z_axis)],
    )
    owns, mates = [], []
    for own, sent, pair in zip(factors[:2], factors[2:], pairs):
        total = pl.pallas_call(
            pair_kernel,
            out_shape=factor,
            in_specs=[VMEM] * 2,
            out_specs=VMEM,
            input_output_aliases={1: 0},
            compiler_params=PARAMS,
            cost_estimate=pl.CostEstimate(flops=block_rows * depth // 2, bytes_accessed=6 * block_rows * depth, transcendentals=0),
            name="pair_sums",
        )(own, lax.ppermute(sent, ("zq", "zp"), pair))
        owns.append(total)
        mates.append(lax.ppermute(total, "core", [(0, 1), (1, 0)]))
    pieces = lax.axis_size("x")
    partial = pl.pallas_call(
        lambda *refs: product_kernel(senders, pieces, *refs),
        out_shape=jax.ShapeDtypeStruct((block_rows // 2, LANES), jnp.float32),
        in_specs=[SMEM] + [VMEM] * 5,
        out_specs=VMEM,
        scratch_shapes=[pltpu.VMEM((2, 2 * depth, 2 * LANES), jnp.bfloat16)],
        compiler_params=PARAMS,
        name="place_and_multiply",
    )(place, arrived, *owns, *mates)
    parts = lax.all_to_all(
        partial.reshape(block_rows // 8, 4, LANES), ("x", "core", "yh", "zq"), split_axis=0, concat_axis=0, tiled=True
    )
    return pl.pallas_call(
        lambda *refs: last_kernel(pieces, *refs),
        out_shape=jax.ShapeDtypeStruct((4, width), jnp.float32),
        in_specs=[VMEM],
        out_specs=VMEM,
        compiler_params=PARAMS,
        name="sum_parts",
    )(parts.reshape(block_rows // 2, LANES))


def solution(mesh):
    fine = Mesh(mesh.devices.reshape(2, 4, 2, 8, 2, 4), ("yh", "zq", "zp", "x", "core", "yl"))
    in_specs = (
        P(("x", "core", "yl"), None),
        P(("x", "core", "yl"), None),
        P(("x", "core", "yl")),
        P(("yh", "zq", "zp"), None, "yl", ("x", "core")),
        P(("yh", "zq", "zp")),
    )
    out_specs = P(("yl", "x", "core", "yh", "zq", "zp"), None)
    return jax.shard_map(per_device, mesh=fine, in_specs=in_specs, out_specs=out_specs, check_vma=False)
```

```python
import math

import jax
import jax.numpy as jnp
from jax import lax
from jax.experimental import pallas as pl
from jax.experimental.pallas import tpu as pltpu
from jax.sharding import Mesh, PartitionSpec as P

POLES = 64
pole_radius = 1.5
weight_scale = 0.3

LANES = 128
SLOTS = 8
VMEM = pl.BlockSpec(memory_space=pltpu.VMEM)
SMEM = pl.BlockSpec(memory_space=pltpu.SMEM)
ANY = pl.BlockSpec(memory_space=pl.ANY)
INPUTS = pltpu.CompilerParams(vmem_limit_bytes=56 * 1024 * 1024)
PARAMS = pltpu.CompilerParams(vmem_limit_bytes=40 * 1024 * 1024)


def iota(shape, axis):
    return lax.broadcasted_iota(jnp.int32, shape, axis)


def pack_kernel(rows_axis, cols_axis, *refs):
    ham, mar, owner, sems = refs[4:]
    out_ref = refs[3]
    share, width = ham.shape
    shift = (share * cols_axis).bit_length() - 1
    copies = [pltpu.make_async_copy(ref, to, sems.at[i]) for i, (ref, to) in enumerate(zip(refs[:3], (ham, mar, owner)))]
    for copy in reversed(copies):
        copy.start()
    copies[2].wait()
    own_r = jnp.broadcast_to(owner[...].astype(jnp.float32), (share, share))
    own_c = jnp.sum(jnp.where(iota((share, share), 0) == iota((share, share), 1), own_r, 0.0), axis=1, keepdims=True)
    own_c = jnp.broadcast_to(own_c, (share, share)).astype(jnp.int32)
    own_r = own_r.astype(jnp.int32)
    same = (own_r >> shift) == (own_c >> shift)
    first, second = iota((share, share), 0), iota((share, share), 1)
    rank_r = jnp.sum(jnp.where(same & (first < second), 1.0, 0.0), axis=0, keepdims=True)
    rank_c = jnp.sum(jnp.where(same & (second < first), 1.0, 0.0), axis=1, keepdims=True)
    slot_r = (own_r[:1] >> shift) * SLOTS + rank_r.astype(jnp.int32)
    slot_c = (own_c[:, :1] >> shift) * SLOTS + rank_c.astype(jnp.int32)
    total = rows_axis * SLOTS
    packer = jnp.where(iota((total, share), 0) == jnp.broadcast_to(slot_r, (total, share)), 1.0, 0.0)
    within = (own_c[:, :1] & ((1 << shift) - 1)) + 1
    labels = jnp.where(
        iota((share, total), 1) == jnp.broadcast_to(slot_c, (share, total)),
        jnp.broadcast_to(within, (share, total)).astype(jnp.float32),
        0.0,
    )
    labels = jnp.sum(labels, axis=0, keepdims=True)
    chunk = 2 * width // LANES * SLOTS + 1
    for target in range(rows_axis * cols_axis):
        base = (target + 1) * chunk - 1
        out_ref[base : base + 1, :] = labels
    wide = 2 * SLOTS
    for which, ref in enumerate((ham, mar)):
        copies[which].wait()
        packed = jnp.dot(packer, ref[...], precision=lax.Precision.HIGHEST, preferred_element_type=jnp.float32)
        for row in range(rows_axis):
            x, core = divmod(row, 2)
            tile = packed[x * wide : (x + 1) * wide, core * LANES : (core + 1) * LANES]
            for col in range(cols_axis):
                base = (row * cols_axis + col) * chunk + which * wide
                out_ref[base : base + wide, :] = tile


def split(value):
    high = value.astype(jnp.bfloat16)
    return high, (value - high.astype(jnp.float32)).astype(jnp.bfloat16)


def left_kernel(place_ref, coef_ref, blocks_ref, *out_refs):
    rows, depth = blocks_ref.shape[1:]
    piece = rows // 16
    odd_here = place_ref[2] == 1
    for index in range(16):
        x, core = divmod(index, 2)
        re = blocks_ref[0, index * piece : (index + 1) * piece, :]
        im = blocks_ref[1, index * piece : (index + 1) * piece, :]
        for which in range(2):
            value = (coef_ref[2 * which] * re + coef_ref[2 * which + 1] * im).reshape(piece // 16, 2, 8, depth)
            first, second = value[:, 0], value[:, 1]
            upper = iota(first.shape, 1) < 4
            even = jnp.where(upper, first, pltpu.roll(second, 4, 1)).reshape(piece // 2, depth)
            odd = jnp.where(upper, pltpu.roll(first, 4, 1), second).reshape(piece // 2, depth)
            at = (slice(x * piece // 2, (x + 1) * piece // 2), slice(which * depth, (which + 1) * depth))
            out_refs[core][at] = jnp.where(odd_here, odd, even)
            out_refs[2 + core][at] = jnp.where(odd_here, even, odd)


def pair_kernel(own_ref, other_ref, sum_ref):
    sum_ref[...] = own_ref[...] + other_ref[...]


def product_kernel(senders, pieces, place_ref, rows_ref, own0, own1, mate0, mate1, out_ref, panel_ref):
    chunk = rows_ref.shape[0] // senders
    depth = panel_ref.shape[1] // 2
    labels = rows_ref[pl.ds(chunk - 1, senders, stride=chunk), :]
    lane = iota((senders, LANES), 1)
    wanted = (iota((senders, depth), 1) + 1).astype(jnp.float32)
    for block in range(2):
        places = []
        for slot in range(SLOTS):
            at = (2 * place_ref[0] + block) * SLOTS + slot
            label = jnp.sum(jnp.where(lane == at, labels, 0.0), axis=1, keepdims=True)
            places.append(jnp.where(jnp.broadcast_to(label, (senders, depth)) == wanted, 1.0, 0.0))
        places = jnp.concatenate(places, axis=0).astype(jnp.bfloat16)
        for which in range(2):
            start = (2 * which + block) * SLOTS
            values = [rows_ref[pl.ds(start + slot, senders, stride=chunk), :] for slot in range(SLOTS)]
            parts = jnp.concatenate(split(jnp.concatenate(values, axis=0)), axis=1)
            placed = lax.dot_general(places, parts, (((0,), (0,)), ((), ())), preferred_element_type=jnp.float32)
            panel_ref[block, which * depth : (which + 1) * depth, :] = placed.astype(jnp.bfloat16)
    for core in range(2):

        @pl.when(place_ref[1] == core)
        def _():
            totals = []
            for pair in ((own0, mate0), (own1, mate1)):
                total = None
                for block in range(2):
                    high, low = split(pair[block ^ core][...])
                    panel = panel_ref[block]
                    both = jnp.dot(high, panel, preferred_element_type=jnp.float32)
                    more = jnp.dot(low, panel[:, :LANES], preferred_element_type=jnp.float32)
                    term = both[:, :LANES] + (both[:, LANES:] + more)
                    total = term if total is None else total + term
                totals.append(total.reshape(pieces, 2, 2, 8, LANES))
            upper = iota(totals[0].shape, 3) < 4
            even = jnp.where(upper, totals[0], pltpu.roll(totals[1], 4, 3))
            odd = jnp.where(upper, pltpu.roll(totals[0], 4, 3), totals[1])
            for z in range(2):
                for yh in range(2):
                    out_ref[:, 2 * z, yh] = even[:, yh, z]
                    out_ref[:, 2 * z + 1, yh] = odd[:, yh, z]


def sum_kernel(place_ref, parts_ref, here_ref, there_ref):
    total = jnp.sum(parts_ref[...], axis=0)
    first = place_ref[3] == 0
    here_ref[...] = jnp.where(first, total[:8], total[8:])
    there_ref[...] = jnp.where(first, total[8:], total[:8])


def halves_kernel(place_ref, here_ref, other_ref, own_ref, mate_ref):
    total = here_ref[...] + other_ref[...]
    first = place_ref[1] == 0
    own_ref[...] = jnp.where(first, total[:4], total[4:])
    mate_ref[...] = jnp.where(first, total[4:], total[:4])


def last_kernel(place_ref, own_ref, other_ref, out_ref):
    first = place_ref[1] == 0
    own, other = own_ref[...], other_ref[...]
    out_ref[:, :LANES] = jnp.where(first, own, other)
    out_ref[:, LANES:] = jnp.where(first, other, own)


def per_device(hamiltonian, margin, owner, inverse_blocks, pole_index):
    rows_axis = lax.axis_size("x") * lax.axis_size("core")
    cols_axis = lax.axis_size("yl")
    share, width = hamiltonian.shape
    senders = rows_axis * cols_axis
    chunk = 2 * width // LANES * SLOTS + 1
    packed = pl.pallas_call(
        lambda *refs: pack_kernel(rows_axis, cols_axis, *refs),
        out_shape=jax.ShapeDtypeStruct((senders * chunk, LANES), jnp.float32),
        in_specs=[ANY] * 3,
        out_specs=VMEM,
        scratch_shapes=[
            pltpu.VMEM((share, width), jnp.float32),
            pltpu.VMEM((share, width), jnp.float32),
            pltpu.VMEM((1, share), jnp.int32),
            pltpu.SemaphoreType.DMA((3,)),
        ],
        compiler_params=INPUTS,
        name="pack_rows",
    )(hamiltonian, margin, owner.reshape(1, share))
    arrived = lax.all_to_all(
        packed.reshape(senders, 1, chunk * LANES), ("x", "core", "yl"), split_axis=0, concat_axis=0, tiled=True
    ).reshape(senders * chunk, LANES)

    theta = math.pi * (pole_index[0].astype(jnp.float32) + 0.5) / POLES
    energy, damping = pole_radius * jnp.cos(theta), pole_radius * jnp.sin(theta)
    weight_re, weight_im = weight_scale * jnp.cos(theta), weight_scale * jnp.sin(theta)
    shifted_re = weight_re * energy - weight_im * damping
    shifted_im = weight_re * damping + weight_im * energy
    coefs = jnp.stack([-weight_im, -weight_re, shifted_im, shifted_re])
    block_rows, depth = inverse_blocks.shape[2:]
    core = lax.axis_index("core")
    place = jnp.stack(
        [lax.axis_index("x"), core, lax.axis_index("zp"), lax.axis_index("yh")]
    ).astype(jnp.int32)
    factor = jax.ShapeDtypeStruct((block_rows // 4, 2 * depth), jnp.float32)
    factors = pl.pallas_call(
        left_kernel,
        out_shape=(factor,) * 4,
        in_specs=[SMEM, SMEM, VMEM],
        out_specs=(VMEM,) * 4,
        compiler_params=PARAMS,
        cost_estimate=pl.CostEstimate(flops=4 * block_rows * depth, bytes_accessed=16 * block_rows * depth, transcendentals=0),
        name="left_factors",
    )(place, coefs, inverse_blocks[0])
    z_axis = lax.axis_size("zq") * lax.axis_size("zp")
    pairs = (
        [(i, i ^ 1) for i in range(z_axis)],
        [(i, (i - 1 if i % 2 == 0 else i + 1) % z_axis) for i in range(z_axis)],
    )
    owns, mates = [], []
    for own, sent, pair in zip(factors[:2], factors[2:], pairs):
        total = pl.pallas_call(
            pair_kernel,
            out_shape=factor,
            in_specs=[VMEM] * 2,
            out_specs=VMEM,
            input_output_aliases={1: 0},
            compiler_params=PARAMS,
            cost_estimate=pl.CostEstimate(flops=block_rows * depth // 2, bytes_accessed=6 * block_rows * depth, transcendentals=0),
            name="pair_sums",
        )(own, lax.ppermute(sent, ("zq", "zp"), pair))
        owns.append(total)
        mates.append(lax.ppermute(total, "core", [(0, 1), (1, 0)]))
    pieces = lax.axis_size("x")
    partial = pl.pallas_call(
        lambda *refs: product_kernel(senders, pieces, *refs),
        out_shape=jax.ShapeDtypeStruct((pieces, 4, 2, 8, LANES), jnp.float32),
        in_specs=[SMEM] + [VMEM] * 5,
        out_specs=VMEM,
        scratch_shapes=[pltpu.VMEM((2, 2 * depth, 2 * LANES), jnp.bfloat16)],
        compiler_params=PARAMS,
        name="place_and_multiply",
    )(place, arrived, *owns, *mates)
    parts = lax.all_to_all(
        partial.reshape(block_rows // 32, 16, LANES), ("x", "zq"), split_axis=0, concat_axis=0, tiled=True
    )
    swap = [(0, 1), (1, 0)]
    tile = jax.ShapeDtypeStruct((8, LANES), jnp.float32)
    here, there = pl.pallas_call(
        sum_kernel,
        out_shape=(tile, tile),
        in_specs=[SMEM, VMEM],
        out_specs=(VMEM, VMEM),
        compiler_params=PARAMS,
        name="sum_parts",
    )(place, parts)
    tile = jax.ShapeDtypeStruct((4, LANES), jnp.float32)
    own, mate = pl.pallas_call(
        halves_kernel,
        out_shape=(tile, tile),
        in_specs=[SMEM, VMEM, VMEM],
        out_specs=(VMEM, VMEM),
        compiler_params=PARAMS,
        name="sum_over_y",
    )(place, here, lax.ppermute(there, "yh", swap))
    return pl.pallas_call(
        last_kernel,
        out_shape=jax.ShapeDtypeStruct((4, width), jnp.float32),
        in_specs=[SMEM, VMEM, VMEM],
        out_specs=VMEM,
        compiler_params=PARAMS,
        name="join_columns",
    )(place, own, lax.ppermute(mate, "core", swap))


def solution(mesh):
    fine = Mesh(mesh.devices.reshape(2, 4, 2, 8, 2, 4), ("yh", "zq", "zp", "x", "core", "yl"))
    in_specs = (
        P(("x", "core", "yl"), None),
        P(("x", "core", "yl"), None),
        P(("x", "core", "yl")),
        P(("yh", "zq", "zp"), None, "yl", ("x", "core")),
        P(("yh", "zq", "zp")),
    )
    out_specs = P(("yl", "x", "core", "yh", "zq", "zp"), None)
    return jax.shard_map(per_device, mesh=fine, in_specs=in_specs, out_specs=out_specs, check_vma=False)
```

```python
import math

import jax
import jax.numpy as jnp
from jax import lax
from jax.experimental import pallas as pl
from jax.experimental.pallas import tpu as pltpu
from jax.sharding import Mesh, PartitionSpec as P

POLES = 64
pole_radius = 1.5
weight_scale = 0.3

LANES = 128
SLOTS = 8
VMEM = pl.BlockSpec(memory_space=pltpu.VMEM)
SMEM = pl.BlockSpec(memory_space=pltpu.SMEM)
ANY = pl.BlockSpec(memory_space=pl.ANY)
INPUTS = pltpu.CompilerParams(vmem_limit_bytes=56 * 1024 * 1024)
PARAMS = pltpu.CompilerParams(vmem_limit_bytes=40 * 1024 * 1024)


def iota(shape, axis):
    return lax.broadcasted_iota(jnp.int32, shape, axis)


def pack_kernel(rows_axis, cols_axis, place_ref, ham_ref, mar_ref, owner_ref, out_ref, held, owner, sems):
    share, width = held.shape
    shift = (share * cols_axis).bit_length() - 1
    labels_copy = pltpu.make_async_copy(owner_ref, owner, sems.at[0])
    labels_copy.start()
    for which, ref in enumerate((ham_ref, mar_ref)):

        @pl.when(place_ref[2] == which)
        def _():
            pltpu.make_async_copy(ref, held, sems.at[1]).start()

    labels_copy.wait()
    own_r = jnp.broadcast_to(owner[...].astype(jnp.float32), (share, share))
    own_c = jnp.sum(jnp.where(iota((share, share), 0) == iota((share, share), 1), own_r, 0.0), axis=1, keepdims=True)
    own_c = jnp.broadcast_to(own_c, (share, share)).astype(jnp.int32)
    own_r = own_r.astype(jnp.int32)
    same = (own_r >> shift) == (own_c >> shift)
    first, second = iota((share, share), 0), iota((share, share), 1)
    rank_r = jnp.sum(jnp.where(same & (first < second), 1.0, 0.0), axis=0, keepdims=True)
    rank_c = jnp.sum(jnp.where(same & (second < first), 1.0, 0.0), axis=1, keepdims=True)
    slot_r = (own_r[:1] >> shift) * SLOTS + rank_r.astype(jnp.int32)
    slot_c = (own_c[:, :1] >> shift) * SLOTS + rank_c.astype(jnp.int32)
    total = rows_axis * SLOTS
    packer = jnp.where(iota((total, share), 0) == jnp.broadcast_to(slot_r, (total, share)), 1.0, 0.0)
    within = (own_c[:, :1] & ((1 << shift) - 1)) + 1
    labels = jnp.where(
        iota((share, total), 1) == jnp.broadcast_to(slot_c, (share, total)),
        jnp.broadcast_to(within, (share, total)).astype(jnp.float32),
        0.0,
    )
    labels = jnp.sum(labels, axis=0, keepdims=True)
    chunk = width // LANES * SLOTS + 1
    for target in range(rows_axis * cols_axis):
        base = (target + 1) * chunk - 1
        out_ref[base : base + 1, :] = labels
    pltpu.make_async_copy(ham_ref, held, sems.at[1]).wait()
    packed = jnp.dot(packer, held[...], precision=lax.Precision.HIGHEST, preferred_element_type=jnp.float32)
    for part in range(width // LANES):
        for row in range(rows_axis):
            tile = packed[row * SLOTS : (row + 1) * SLOTS, part * LANES : (part + 1) * LANES]
            for col in range(cols_axis):
                base = (row * cols_axis + col) * chunk + part * SLOTS
                out_ref[base : base + SLOTS, :] = tile


def split(value):
    high = value.astype(jnp.bfloat16)
    return high, (value - high.astype(jnp.float32)).astype(jnp.bfloat16)


def left_kernel(place_ref, coef_ref, blocks_ref, *out_refs):
    rows, depth = blocks_ref.shape[1:]
    piece = rows // 16
    odd_here = place_ref[2] == 1
    for index in range(16):
        x, core = divmod(index, 2)
        re = blocks_ref[0, index * piece : (index + 1) * piece, :]
        im = blocks_ref[1, index * piece : (index + 1) * piece, :]
        for which in range(2):
            value = (coef_ref[2 * which] * re + coef_ref[2 * which + 1] * im).reshape(piece // 16, 2, 8, depth)
            first, second = value[:, 0], value[:, 1]
            upper = iota(first.shape, 1) < 4
            even = jnp.where(upper, first, pltpu.roll(second, 4, 1)).reshape(piece // 2, depth)
            odd = jnp.where(upper, pltpu.roll(first, 4, 1), second).reshape(piece // 2, depth)
            at = (slice(x * piece // 2, (x + 1) * piece // 2), slice(which * depth, (which + 1) * depth))
            out_refs[core][at] = jnp.where(odd_here, odd, even)
            out_refs[2 + core][at] = jnp.where(odd_here, even, odd)


def pair_kernel(own_ref, other_ref, high_ref, low_ref):
    high_ref[...], low_ref[...] = split(own_ref[...] + other_ref[...])


def store_chunks(out_ref, value):
    pairs = value.shape[0] // 8
    left = value[:, :LANES].reshape(pairs, 8, LANES)
    right = value[:, LANES:].reshape(pairs, 8, LANES)
    upper = iota((pairs, 8, LANES), 1) < 4
    out_ref[:, 0] = jnp.where(upper, left, pltpu.roll(right, 4, 1))
    out_ref[:, 1] = jnp.where(upper, pltpu.roll(left, 4, 1), right)


def place_kernel(senders, place_ref, rows_ref, out_ref):
    chunk = rows_ref.shape[0] // senders
    depth = out_ref.shape[0]
    labels = rows_ref[pl.ds(chunk - 1, senders, stride=chunk), :]
    lane = iota((senders, LANES), 1)
    wanted = (iota((senders, depth), 1) + 1).astype(jnp.float32)
    places = []
    for slot in range(SLOTS):
        label = jnp.sum(jnp.where(lane == place_ref[0] * SLOTS + slot, labels, 0.0), axis=1, keepdims=True)
        places.append(jnp.where(jnp.broadcast_to(label, (senders, depth)) == wanted, 1.0, 0.0))
    places = jnp.concatenate(places, axis=0).astype(jnp.bfloat16)
    for part in range((chunk - 1) // SLOTS):
        values = [rows_ref[pl.ds(part * SLOTS + slot, senders, stride=chunk), :] for slot in range(SLOTS)]
        pieces = jnp.concatenate(split(jnp.concatenate(values, axis=0)), axis=1)
        placed = lax.dot_general(places, pieces, (((0,), (0,)), ((), ())), preferred_element_type=jnp.float32)
        out_ref[:, part * LANES : (part + 1) * LANES] = placed[:, :LANES] + placed[:, LANES:]


def multiply(out_ref, which, highs, lows, panels):
    dot = lambda a, b: jnp.dot(a, b, preferred_element_type=jnp.float32)
    for index in range(2):

        @pl.when(which == index)
        def _():
            total = None
            for field, (panel_high, panel_low) in enumerate(panels):
                depth = panel_high.shape[0]
                columns = slice(field * depth, (field + 1) * depth)
                high, low = highs[index][:, columns], lows[index][:, columns]
                term = dot(high, panel_high) + (dot(low, panel_high) + dot(high, panel_low))
                total = term if total is None else total + term
            store_chunks(out_ref, total)


def ordered(place_ref, mine_ref, other_ref):
    even = place_ref[2] == 0
    mine, other = mine_ref[...], other_ref[...]
    return split(jnp.where(even, mine, other)), split(jnp.where(even, other, mine))


def first_kernel(place_ref, mine_ref, other_ref, high0, low0, high1, low1, out_ref):
    multiply(out_ref, 1 - place_ref[1], (high0, high1), (low0, low1), ordered(place_ref, mine_ref, other_ref))


def second_kernel(place_ref, mine_ref, other_ref, high0, low0, high1, low1, out_ref):
    multiply(out_ref, place_ref[1], (high0, high1), (low0, low1), ordered(place_ref, mine_ref, other_ref))


def last_kernel(parts_ref, out_ref):
    total = jnp.sum(parts_ref[...], axis=0)
    out_ref[:, :LANES] = total[:4]
    out_ref[:, LANES:] = total[4:]


def per_device(hamiltonian, margin, owner, inverse_blocks, pole_index):
    rows_axis = lax.axis_size("x") * lax.axis_size("core")
    cols_axis = lax.axis_size("yl")
    share, width = hamiltonian.shape
    senders = rows_axis * cols_axis
    chunk = width // LANES * SLOTS + 1
    core = lax.axis_index("core")
    place = jnp.stack(
        [lax.axis_index("x") * lax.axis_size("core") + core, core, lax.axis_index("zp")]
    ).astype(jnp.int32)
    packed = pl.pallas_call(
        lambda *refs: pack_kernel(rows_axis, cols_axis, *refs),
        out_shape=jax.ShapeDtypeStruct((senders * chunk, LANES), jnp.float32),
        in_specs=[SMEM] + [ANY] * 3,
        out_specs=VMEM,
        scratch_shapes=[
            pltpu.VMEM((share, width), jnp.float32),
            pltpu.VMEM((1, share), jnp.int32),
            pltpu.SemaphoreType.DMA((2,)),
        ],
        compiler_params=INPUTS,
        name="pack_rows",
    )(place, hamiltonian, margin, owner.reshape(1, share))
    arrived = lax.all_to_all(
        packed.reshape(senders, 1, chunk * LANES), ("x", "core", "yl"), split_axis=0, concat_axis=0, tiled=True
    ).reshape(senders * chunk, LANES)

    theta = math.pi * (pole_index[0].astype(jnp.float32) + 0.5) / POLES
    energy, damping = pole_radius * jnp.cos(theta), pole_radius * jnp.sin(theta)
    weight_re, weight_im = weight_scale * jnp.cos(theta), weight_scale * jnp.sin(theta)
    shifted_re = weight_re * energy - weight_im * damping
    shifted_im = weight_re * damping + weight_im * energy
    coefs = jnp.stack([-weight_im, -weight_re, shifted_im, shifted_re])
    block_rows, depth = inverse_blocks.shape[2:]
    factor = jax.ShapeDtypeStruct((block_rows // 4, 2 * depth), jnp.float32)
    factors = pl.pallas_call(
        left_kernel,
        out_shape=(factor,) * 4,
        in_specs=[SMEM, SMEM, VMEM],
        out_specs=(VMEM,) * 4,
        compiler_params=PARAMS,
        cost_estimate=pl.CostEstimate(flops=4 * block_rows * depth, bytes_accessed=16 * block_rows * depth, transcendentals=0),
        name="left_factors",
    )(place, coefs, inverse_blocks[0])
    z_axis = lax.axis_size("zq") * lax.axis_size("zp")
    pairs = (
        [(i, i ^ 1) for i in range(z_axis)],
        [(i, (i - 1 if i % 2 == 0 else i + 1) % z_axis) for i in range(z_axis)],
    )
    part = jax.ShapeDtypeStruct(factor.shape, jnp.bfloat16)
    summed = []
    for own, sent, pair in zip(factors[:2], factors[2:], pairs):
        summed += pl.pallas_call(
            pair_kernel,
            out_shape=(part, part),
            in_specs=[VMEM] * 2,
            out_specs=(VMEM, VMEM),
            compiler_params=PARAMS,
            cost_estimate=pl.CostEstimate(flops=block_rows * depth, bytes_accessed=6 * block_rows * depth, transcendentals=0),
            name="pair_sums",
        )(own, lax.ppermute(sent, ("zq", "zp"), pair))
    chunks = jax.ShapeDtypeStruct((block_rows // 32, 2, 8, LANES), jnp.float32)
    mine = pl.pallas_call(
        lambda *refs: place_kernel(senders, *refs),
        out_shape=jax.ShapeDtypeStruct((depth, width), jnp.float32),
        in_specs=[SMEM, VMEM],
        out_specs=VMEM,
        compiler_params=PARAMS,
        name="place_rows",
    )(place, arrived)
    other = lax.ppermute(mine, "zp", [(0, 1), (1, 0)])
    sent = pl.pallas_call(
        first_kernel,
        out_shape=chunks,
        in_specs=[SMEM] + [VMEM] * 6,
        out_specs=VMEM,
        compiler_params=PARAMS,
        name="multiply_other",
    )(place, mine, other, *summed)
    received = lax.ppermute(sent, "core", [(0, 1), (1, 0)])
    kept = pl.pallas_call(
        second_kernel,
        out_shape=chunks,
        in_specs=[SMEM] + [VMEM] * 6,
        out_specs=VMEM,
        compiler_params=PARAMS,
        cost_estimate=pl.CostEstimate(flops=3 * block_rows * depth * width, bytes_accessed=block_rows * depth * 4, transcendentals=0),
        name="multiply_own",
    )(place, mine, other, *summed)
    both = (kept + received).reshape(block_rows // 16, 8, LANES)
    parts = lax.all_to_all(both, ("x", "yh", "zq"), split_axis=0, concat_axis=0, tiled=True)
    return pl.pallas_call(
        last_kernel,
        out_shape=jax.ShapeDtypeStruct((4, width), jnp.float32),
        in_specs=[VMEM],
        out_specs=VMEM,
        compiler_params=PARAMS,
        name="sum_parts",
    )(parts)


def solution(mesh):
    fine = Mesh(mesh.devices.reshape(2, 4, 2, 8, 2, 4), ("yh", "zq", "zp", "x", "core", "yl"))
    in_specs = (
        P(("x", "core", "yl"), None),
        P(("x", "core", "yl"), None),
        P(("x", "core", "yl")),
        P(("yh", "zq", "zp"), None, "yl", ("x", "core")),
        P(("yh", "zq", "zp")),
    )
    out_specs = P(("yl", "x", "core", "yh", "zq", "zp"), None)
    return jax.shard_map(per_device, mesh=fine, in_specs=in_specs, out_specs=out_specs, check_vma=False)
```

```python
import math

import jax
import jax.numpy as jnp
from jax import lax
from jax.experimental import pallas as pl
from jax.experimental.pallas import tpu as pltpu
from jax.sharding import Mesh, PartitionSpec as P

POLES = 64
pole_radius = 1.5
weight_scale = 0.3

LANES = 128
PANEL_FLOPS = 5000000000
SLOTS = 8
VMEM = pl.BlockSpec(memory_space=pltpu.VMEM)
SMEM = pl.BlockSpec(memory_space=pltpu.SMEM)
ANY = pl.BlockSpec(memory_space=pl.ANY)
INPUTS = pltpu.CompilerParams(vmem_limit_bytes=56 * 1024 * 1024)
PARAMS = pltpu.CompilerParams(vmem_limit_bytes=40 * 1024 * 1024)


def iota(shape, axis):
    return lax.broadcasted_iota(jnp.int32, shape, axis)


def pack_kernel(rows_axis, cols_axis, ham_ref, mar_ref, owner_ref, out_ref, held, owner, sems):
    share, width = held.shape
    shift = (share * cols_axis).bit_length() - 1
    labels_copy = pltpu.make_async_copy(owner_ref, owner, sems.at[0])
    labels_copy.start()
    for which, ref in enumerate((ham_ref, mar_ref)):

        @pl.when(lax.axis_index("zp") == which)
        def _():
            pltpu.make_async_copy(ref, held, sems.at[1]).start()

    labels_copy.wait()
    own_r = jnp.broadcast_to(owner[...].astype(jnp.float32), (share, share))
    own_c = jnp.sum(jnp.where(iota((share, share), 0) == iota((share, share), 1), own_r, 0.0), axis=1, keepdims=True)
    own_c = jnp.broadcast_to(own_c, (share, share)).astype(jnp.int32)
    own_r = own_r.astype(jnp.int32)
    same = (own_r >> shift) == (own_c >> shift)
    first, second = iota((share, share), 0), iota((share, share), 1)
    rank_r = jnp.sum(jnp.where(same & (first < second), 1.0, 0.0), axis=0, keepdims=True)
    rank_c = jnp.sum(jnp.where(same & (second < first), 1.0, 0.0), axis=1, keepdims=True)
    slot_r = (own_r[:1] >> shift) * SLOTS + rank_r.astype(jnp.int32)
    slot_c = (own_c[:, :1] >> shift) * SLOTS + rank_c.astype(jnp.int32)
    total = rows_axis * SLOTS
    packer = jnp.where(iota((total, share), 0) == jnp.broadcast_to(slot_r, (total, share)), 1.0, 0.0)
    within = (own_c[:, :1] & ((1 << shift) - 1)) + 1
    labels = jnp.where(
        iota((share, total), 1) == jnp.broadcast_to(slot_c, (share, total)),
        jnp.broadcast_to(within, (share, total)).astype(jnp.float32),
        0.0,
    )
    labels = jnp.sum(labels, axis=0, keepdims=True)
    chunk = width // LANES * SLOTS + 1
    for target in range(rows_axis * cols_axis):
        base = (target + 1) * chunk - 1
        out_ref[base : base + 1, :] = labels
    pltpu.make_async_copy(ham_ref, held, sems.at[1]).wait()
    packed = jnp.dot(packer, held[...], precision=lax.Precision.HIGHEST, preferred_element_type=jnp.float32)
    wide = 2 * SLOTS
    for row in range(rows_axis):
        x, core = divmod(row, 2)
        tile = packed[x * wide : (x + 1) * wide, core * LANES : (core + 1) * LANES]
        for col in range(cols_axis):
            base = (row * cols_axis + col) * chunk
            out_ref[base : base + wide, :] = tile


def split(value):
    high = value.astype(jnp.bfloat16)
    return high, (value - high.astype(jnp.float32)).astype(jnp.bfloat16)


def left_kernel(place_ref, coef_ref, blocks_ref, *out_refs):
    rows, depth = blocks_ref.shape[1:]
    piece = rows // 16
    odd_here = place_ref[2] == 1
    for index in range(16):
        x, core = divmod(index, 2)
        re = blocks_ref[0, index * piece : (index + 1) * piece, :]
        im = blocks_ref[1, index * piece : (index + 1) * piece, :]
        for which in range(2):
            value = (coef_ref[2 * which] * re + coef_ref[2 * which + 1] * im).reshape(piece // 16, 2, 8, depth)
            first, second = value[:, 0], value[:, 1]
            upper = iota(first.shape, 1) < 4
            even = jnp.where(upper, first, pltpu.roll(second, 4, 1)).reshape(piece // 2, depth)
            odd = jnp.where(upper, pltpu.roll(first, 4, 1), second).reshape(piece // 2, depth)
            at = (slice(x * piece // 2, (x + 1) * piece // 2), slice(which * depth, (which + 1) * depth))
            out_refs[core][at] = jnp.where(odd_here, odd, even)
            out_refs[2 + core][at] = jnp.where(odd_here, even, odd)


def pair_kernel(own_ref, other_ref, sum_ref):
    sum_ref[...] = own_ref[...] + other_ref[...]


def place_kernel(senders, place_ref, rows_ref, out_ref):
    chunk = rows_ref.shape[0] // senders
    depth = out_ref.shape[0] // 2
    labels = rows_ref[pl.ds(chunk - 1, senders, stride=chunk), :]
    lane = iota((senders, LANES), 1)
    wanted = (iota((senders, depth), 1) + 1).astype(jnp.float32)
    for block in range(2):
        places = []
        for slot in range(SLOTS):
            at = (2 * place_ref[0] + block) * SLOTS + slot
            label = jnp.sum(jnp.where(lane == at, labels, 0.0), axis=1, keepdims=True)
            places.append(jnp.where(jnp.broadcast_to(label, (senders, depth)) == wanted, 1.0, 0.0))
        places = jnp.concatenate(places, axis=0).astype(jnp.bfloat16)
        values = [rows_ref[pl.ds(block * SLOTS + slot, senders, stride=chunk), :] for slot in range(SLOTS)]
        parts = jnp.concatenate(split(jnp.concatenate(values, axis=0)), axis=1)
        placed = lax.dot_general(places, parts, (((0,), (0,)), ((), ())), preferred_element_type=jnp.float32)
        out_ref[block * depth : (block + 1) * depth, :] = placed[:, :LANES] + placed[:, LANES:]


def panel_kernel(place_ref, mine_ref, other_ref, panel_ref):
    depth = panel_ref.shape[1] // 2
    even = place_ref[2] == 0
    for block in range(2):
        rows = slice(block * depth, (block + 1) * depth)
        mine, other = mine_ref[rows], other_ref[rows]
        for which, value in enumerate((jnp.where(even, mine, other), jnp.where(even, other, mine))):
            panel_ref[block, which * depth : (which + 1) * depth, :] = jnp.concatenate(split(value), axis=1)


def product_kernel(pieces, place_ref, panel_ref, own0, own1, mate0, mate1, out_ref):
    for core in range(2):

        @pl.when(place_ref[1] == core)
        def _():
            for row_core, pair in enumerate(((own0, mate0), (own1, mate1))):
                total = None
                for block in range(2):
                    high, low = split(pair[block ^ core][...])
                    panel = panel_ref[block]
                    both = jnp.dot(high, panel, preferred_element_type=jnp.float32)
                    more = jnp.dot(low, panel[:, :LANES], preferred_element_type=jnp.float32)
                    term = both[:, :LANES] + (both[:, LANES:] + more)
                    total = term if total is None else total + term
                size = total.shape[0] // pieces
                for x in range(pieces):
                    start = (2 * x + row_core) * size
                    out_ref[start : start + size, :] = total[x * size : (x + 1) * size]


def last_kernel(pieces, parts_ref, out_ref):
    parts = parts_ref[...].reshape(pieces, 2, -1, 8, LANES)
    total = jnp.sum(jnp.sum(parts, axis=2), axis=0)
    total = total[:, :4] + total[:, 4:]
    out_ref[:, :LANES] = total[0]
    out_ref[:, LANES:] = total[1]


def per_device(hamiltonian, margin, owner, inverse_blocks, pole_index):
    rows_axis = lax.axis_size("x") * lax.axis_size("core")
    cols_axis = lax.axis_size("yl")
    share, width = hamiltonian.shape
    senders = rows_axis * cols_axis
    chunk = width // LANES * SLOTS + 1
    core = lax.axis_index("core")
    place = jnp.stack(
        [lax.axis_index("x"), core, lax.axis_index("zp")]
    ).astype(jnp.int32)
    packed = pl.pallas_call(
        lambda *refs: pack_kernel(rows_axis, cols_axis, *refs),
        out_shape=jax.ShapeDtypeStruct((senders * chunk, LANES), jnp.float32),
        in_specs=[ANY] * 3,
        out_specs=VMEM,
        scratch_shapes=[
            pltpu.VMEM((share, width), jnp.float32),
            pltpu.VMEM((1, share), jnp.int32),
            pltpu.SemaphoreType.DMA((2,)),
        ],
        compiler_params=INPUTS,
        name="pack_rows",
    )(hamiltonian, margin, owner.reshape(1, share))
    arrived = lax.all_to_all(
        packed.reshape(senders, 1, chunk * LANES), ("x", "core", "yl"), split_axis=0, concat_axis=0, tiled=True
    ).reshape(senders * chunk, LANES)

    theta = math.pi * (pole_index[0].astype(jnp.float32) + 0.5) / POLES
    energy, damping = pole_radius * jnp.cos(theta), pole_radius * jnp.sin(theta)
    weight_re, weight_im = weight_scale * jnp.cos(theta), weight_scale * jnp.sin(theta)
    shifted_re = weight_re * energy - weight_im * damping
    shifted_im = weight_re * damping + weight_im * energy
    coefs = jnp.stack([-weight_im, -weight_re, shifted_im, shifted_re])
    block_rows, depth = inverse_blocks.shape[2:]
    factor = jax.ShapeDtypeStruct((block_rows // 4, 2 * depth), jnp.float32)
    factors = pl.pallas_call(
        left_kernel,
        out_shape=(factor,) * 4,
        in_specs=[SMEM, SMEM, VMEM],
        out_specs=(VMEM,) * 4,
        compiler_params=PARAMS,
        cost_estimate=pl.CostEstimate(flops=4 * block_rows * depth, bytes_accessed=16 * block_rows * depth, transcendentals=0),
        name="left_factors",
    )(place, coefs, inverse_blocks[0])
    z_axis = lax.axis_size("zq") * lax.axis_size("zp")
    pairs = (
        [(i, i ^ 1) for i in range(z_axis)],
        [(i, (i - 1 if i % 2 == 0 else i + 1) % z_axis) for i in range(z_axis)],
    )
    owns, mates = [], []
    for own, sent, pair in zip(factors[:2], factors[2:], pairs):
        total = pl.pallas_call(
            pair_kernel,
            out_shape=factor,
            in_specs=[VMEM] * 2,
            out_specs=VMEM,
            input_output_aliases={1: 0},
            compiler_params=PARAMS,
            cost_estimate=pl.CostEstimate(flops=block_rows * depth // 2, bytes_accessed=6 * block_rows * depth, transcendentals=0),
            name="pair_sums",
        )(own, lax.ppermute(sent, ("zq", "zp"), pair))
        owns.append(total)
        mates.append(lax.ppermute(total, "core", [(0, 1), (1, 0)]))
    mine = pl.pallas_call(
        lambda *refs: place_kernel(senders, *refs),
        out_shape=jax.ShapeDtypeStruct((2 * depth, LANES), jnp.float32),
        in_specs=[SMEM, VMEM],
        out_specs=VMEM,
        compiler_params=PARAMS,
        name="place_rows",
    )(place, arrived)
    other = lax.ppermute(mine, "zp", [(0, 1), (1, 0)])
    panel = pl.pallas_call(
        panel_kernel,
        out_shape=jax.ShapeDtypeStruct((2, 2 * depth, 2 * LANES), jnp.bfloat16),
        in_specs=[SMEM, VMEM, VMEM],
        out_specs=VMEM,
        compiler_params=PARAMS,
        cost_estimate=pl.CostEstimate(flops=PANEL_FLOPS, bytes_accessed=2**20, transcendentals=0),
        name="split_panel",
    )(place, mine, other)
    pieces = lax.axis_size("x")
    partial = pl.pallas_call(
        lambda *refs: product_kernel(pieces, *refs),
        out_shape=jax.ShapeDtypeStruct((block_rows // 2, LANES), jnp.float32),
        in_specs=[SMEM] + [VMEM] * 5,
        out_specs=VMEM,
        compiler_params=PARAMS,
        name="multiply",
    )(place, panel, *owns, *mates)
    parts = lax.all_to_all(
        partial.reshape(block_rows // 8, 4, LANES), ("x", "core", "yh", "zq"), split_axis=0, concat_axis=0, tiled=True
    )
    return pl.pallas_call(
        lambda *refs: last_kernel(pieces, *refs),
        out_shape=jax.ShapeDtypeStruct((4, width), jnp.float32),
        in_specs=[VMEM],
        out_specs=VMEM,
        compiler_params=PARAMS,
        name="sum_parts",
    )(parts.reshape(block_rows // 2, LANES))


def solution(mesh):
    fine = Mesh(mesh.devices.reshape(2, 4, 2, 8, 2, 4), ("yh", "zq", "zp", "x", "core", "yl"))
    in_specs = (
        P(("x", "core", "yl"), None),
        P(("x", "core", "yl"), None),
        P(("x", "core", "yl")),
        P(("yh", "zq", "zp"), None, "yl", ("x", "core")),
        P(("yh", "zq", "zp")),
    )
    out_specs = P(("yl", "x", "core", "yh", "zq", "zp"), None)
    return jax.shard_map(per_device, mesh=fine, in_specs=in_specs, out_specs=out_specs, check_vma=False)
```

```python
import math

import jax
import jax.numpy as jnp
from jax import lax
from jax.experimental import pallas as pl
from jax.experimental.pallas import tpu as pltpu
from jax.sharding import Mesh, PartitionSpec as P

POLES = 64
pole_radius = 1.5
weight_scale = 0.3

LANES = 128
PANEL_FLOPS = 10000000000
SLOTS = 8
VMEM = pl.BlockSpec(memory_space=pltpu.VMEM)
SMEM = pl.BlockSpec(memory_space=pltpu.SMEM)
ANY = pl.BlockSpec(memory_space=pl.ANY)
INPUTS = pltpu.CompilerParams(vmem_limit_bytes=56 * 1024 * 1024)
PARAMS = pltpu.CompilerParams(vmem_limit_bytes=40 * 1024 * 1024)


def iota(shape, axis):
    return lax.broadcasted_iota(jnp.int32, shape, axis)


def pack_kernel(rows_axis, cols_axis, ham_ref, mar_ref, owner_ref, out_ref, held, owner, sems):
    share, width = held.shape
    shift = (share * cols_axis).bit_length() - 1
    labels_copy = pltpu.make_async_copy(owner_ref, owner, sems.at[0])
    labels_copy.start()
    for which, ref in enumerate((ham_ref, mar_ref)):

        @pl.when(lax.axis_index("zp") == which)
        def _():
            pltpu.make_async_copy(ref, held, sems.at[1]).start()

    labels_copy.wait()
    own_r = jnp.broadcast_to(owner[...].astype(jnp.float32), (share, share))
    own_c = jnp.sum(jnp.where(iota((share, share), 0) == iota((share, share), 1), own_r, 0.0), axis=1, keepdims=True)
    own_c = jnp.broadcast_to(own_c, (share, share)).astype(jnp.int32)
    own_r = own_r.astype(jnp.int32)
    same = (own_r >> shift) == (own_c >> shift)
    first, second = iota((share, share), 0), iota((share, share), 1)
    rank_r = jnp.sum(jnp.where(same & (first < second), 1.0, 0.0), axis=0, keepdims=True)
    rank_c = jnp.sum(jnp.where(same & (second < first), 1.0, 0.0), axis=1, keepdims=True)
    slot_r = (own_r[:1] >> shift) * SLOTS + rank_r.astype(jnp.int32)
    slot_c = (own_c[:, :1] >> shift) * SLOTS + rank_c.astype(jnp.int32)
    total = rows_axis * SLOTS
    packer = jnp.where(iota((total, share), 0) == jnp.broadcast_to(slot_r, (total, share)), 1.0, 0.0)
    within = (own_c[:, :1] & ((1 << shift) - 1)) + 1
    labels = jnp.where(
        iota((share, total), 1) == jnp.broadcast_to(slot_c, (share, total)),
        jnp.broadcast_to(within, (share, total)).astype(jnp.float32),
        0.0,
    )
    labels = jnp.sum(labels, axis=0, keepdims=True)
    chunk = width // LANES * SLOTS + 1
    for target in range(rows_axis * cols_axis):
        base = (target + 1) * chunk - 1
        out_ref[base : base + 1, :] = labels
    pltpu.make_async_copy(ham_ref, held, sems.at[1]).wait()
    packed = jnp.dot(packer, held[...], precision=lax.Precision.HIGHEST, preferred_element_type=jnp.float32)
    wide = 2 * SLOTS
    for row in range(rows_axis):
        x, core = divmod(row, 2)
        tile = packed[x * wide : (x + 1) * wide, core * LANES : (core + 1) * LANES]
        for col in range(cols_axis):
            base = (row * cols_axis + col) * chunk
            out_ref[base : base + wide, :] = tile


def split(value):
    high = value.astype(jnp.bfloat16)
    return high, (value - high.astype(jnp.float32)).astype(jnp.bfloat16)


def left_kernel(place_ref, coef_ref, blocks_ref, *out_refs):
    rows, depth = blocks_ref.shape[1:]
    piece = rows // 16
    odd_here = place_ref[2] == 1
    for index in range(16):
        x, core = divmod(index, 2)
        re = blocks_ref[0, index * piece : (index + 1) * piece, :]
        im = blocks_ref[1, index * piece : (index + 1) * piece, :]
        for which in range(2):
            value = (coef_ref[2 * which] * re + coef_ref[2 * which + 1] * im).reshape(piece // 16, 2, 8, depth)
            first, second = value[:, 0], value[:, 1]
            upper = iota(first.shape, 1) < 4
            even = jnp.where(upper, first, pltpu.roll(second, 4, 1)).reshape(piece // 2, depth)
            odd = jnp.where(upper, pltpu.roll(first, 4, 1), second).reshape(piece // 2, depth)
            at = (slice(x * piece // 2, (x + 1) * piece // 2), slice(which * depth, (which + 1) * depth))
            out_refs[core][at] = jnp.where(odd_here, odd, even)
            out_refs[2 + core][at] = jnp.where(odd_here, even, odd)


def pair_kernel(own0, other0, own1, other1, sum_ref):
    rows = own0.shape[0]
    sum_ref[:rows] = own0[...] + other0[...]
    sum_ref[rows:] = own1[...] + other1[...]


def place_kernel(senders, place_ref, rows_ref, out_ref):
    chunk = rows_ref.shape[0] // senders
    depth = out_ref.shape[0] // 2
    labels = rows_ref[pl.ds(chunk - 1, senders, stride=chunk), :]
    lane = iota((senders, LANES), 1)
    wanted = (iota((senders, depth), 1) + 1).astype(jnp.float32)
    for block in range(2):
        places = []
        for slot in range(SLOTS):
            at = (2 * place_ref[0] + block) * SLOTS + slot
            label = jnp.sum(jnp.where(lane == at, labels, 0.0), axis=1, keepdims=True)
            places.append(jnp.where(jnp.broadcast_to(label, (senders, depth)) == wanted, 1.0, 0.0))
        places = jnp.concatenate(places, axis=0).astype(jnp.bfloat16)
        values = [rows_ref[pl.ds(block * SLOTS + slot, senders, stride=chunk), :] for slot in range(SLOTS)]
        parts = jnp.concatenate(split(jnp.concatenate(values, axis=0)), axis=1)
        placed = lax.dot_general(places, parts, (((0,), (0,)), ((), ())), preferred_element_type=jnp.float32)
        out_ref[block * depth : (block + 1) * depth, :] = placed[:, :LANES] + placed[:, LANES:]


def panel_kernel(place_ref, mine_ref, other_ref, panel_ref):
    depth = panel_ref.shape[1] // 2
    even = place_ref[2] == 0
    for block in range(2):
        rows = slice(block * depth, (block + 1) * depth)
        mine, other = mine_ref[rows], other_ref[rows]
        for which, value in enumerate((jnp.where(even, mine, other), jnp.where(even, other, mine))):
            panel_ref[block, which * depth : (which + 1) * depth, :] = jnp.concatenate(split(value), axis=1)


def product_kernel(pieces, place_ref, panel_ref, own_ref, mate_ref, out_ref):
    for core in range(2):

        @pl.when(place_ref[1] == core)
        def _():
            half = own_ref.shape[0] // 2
            for row_core in range(2):
                rows = slice(row_core * half, (row_core + 1) * half)
                total = None
                for block in range(2):
                    high, low = split((own_ref, mate_ref)[block ^ core][rows])
                    panel = panel_ref[block]
                    both = jnp.dot(high, panel, preferred_element_type=jnp.float32)
                    more = jnp.dot(low, panel[:, :LANES], preferred_element_type=jnp.float32)
                    term = both[:, :LANES] + (both[:, LANES:] + more)
                    total = term if total is None else total + term
                size = total.shape[0] // pieces
                for x in range(pieces):
                    start = (2 * x + row_core) * size
                    out_ref[start : start + size, :] = total[x * size : (x + 1) * size]


def last_kernel(pieces, parts_ref, out_ref):
    parts = parts_ref[...].reshape(pieces, 2, -1, 8, LANES)
    total = jnp.sum(jnp.sum(parts, axis=2), axis=0)
    total = total[:, :4] + total[:, 4:]
    out_ref[:, :LANES] = total[0]
    out_ref[:, LANES:] = total[1]


def per_device(hamiltonian, margin, owner, inverse_blocks, pole_index):
    rows_axis = lax.axis_size("x") * lax.axis_size("core")
    cols_axis = lax.axis_size("yl")
    share, width = hamiltonian.shape
    senders = rows_axis * cols_axis
    chunk = width // LANES * SLOTS + 1
    core = lax.axis_index("core")
    place = jnp.stack(
        [lax.axis_index("x"), core, lax.axis_index("zp")]
    ).astype(jnp.int32)
    packed = pl.pallas_call(
        lambda *refs: pack_kernel(rows_axis, cols_axis, *refs),
        out_shape=jax.ShapeDtypeStruct((senders * chunk, LANES), jnp.float32),
        in_specs=[ANY] * 3,
        out_specs=VMEM,
        scratch_shapes=[
            pltpu.VMEM((share, width), jnp.float32),
            pltpu.VMEM((1, share), jnp.int32),
            pltpu.SemaphoreType.DMA((2,)),
        ],
        compiler_params=INPUTS,
        name="pack_rows",
    )(hamiltonian, margin, owner.reshape(1, share))
    arrived = lax.all_to_all(
        packed.reshape(senders, 1, chunk * LANES), ("x", "core", "yl"), split_axis=0, concat_axis=0, tiled=True
    ).reshape(senders * chunk, LANES)

    theta = math.pi * (pole_index[0].astype(jnp.float32) + 0.5) / POLES
    energy, damping = pole_radius * jnp.cos(theta), pole_radius * jnp.sin(theta)
    weight_re, weight_im = weight_scale * jnp.cos(theta), weight_scale * jnp.sin(theta)
    shifted_re = weight_re * energy - weight_im * damping
    shifted_im = weight_re * damping + weight_im * energy
    coefs = jnp.stack([-weight_im, -weight_re, shifted_im, shifted_re])
    block_rows, depth = inverse_blocks.shape[2:]
    factor = jax.ShapeDtypeStruct((block_rows // 4, 2 * depth), jnp.float32)
    factors = pl.pallas_call(
        left_kernel,
        out_shape=(factor,) * 4,
        in_specs=[SMEM, SMEM, VMEM],
        out_specs=(VMEM,) * 4,
        compiler_params=PARAMS,
        cost_estimate=pl.CostEstimate(flops=4 * block_rows * depth, bytes_accessed=16 * block_rows * depth, transcendentals=0),
        name="left_factors",
    )(place, coefs, inverse_blocks[0])
    z_axis = lax.axis_size("zq") * lax.axis_size("zp")
    pairs = (
        [(i, i ^ 1) for i in range(z_axis)],
        [(i, (i - 1 if i % 2 == 0 else i + 1) % z_axis) for i in range(z_axis)],
    )
    others = [lax.ppermute(sent, ("zq", "zp"), pair) for sent, pair in zip(factors[2:], pairs)]
    total = pl.pallas_call(
        pair_kernel,
        out_shape=jax.ShapeDtypeStruct((block_rows // 2, 2 * depth), jnp.float32),
        in_specs=[VMEM] * 4,
        out_specs=VMEM,
        compiler_params=PARAMS,
        cost_estimate=pl.CostEstimate(flops=block_rows * depth, bytes_accessed=12 * block_rows * depth, transcendentals=0),
        name="pair_sums",
    )(factors[0], others[0], factors[1], others[1])
    mate = lax.ppermute(total, "core", [(0, 1), (1, 0)])
    mine = pl.pallas_call(
        lambda *refs: place_kernel(senders, *refs),
        out_shape=jax.ShapeDtypeStruct((2 * depth, LANES), jnp.float32),
        in_specs=[SMEM, VMEM],
        out_specs=VMEM,
        compiler_params=PARAMS,
        name="place_rows",
    )(place, arrived)
    other = lax.ppermute(mine, "zp", [(0, 1), (1, 0)])
    panel = pl.pallas_call(
        panel_kernel,
        out_shape=jax.ShapeDtypeStruct((2, 2 * depth, 2 * LANES), jnp.bfloat16),
        in_specs=[SMEM, VMEM, VMEM],
        out_specs=VMEM,
        compiler_params=PARAMS,
        cost_estimate=pl.CostEstimate(flops=PANEL_FLOPS, bytes_accessed=2**20, transcendentals=0),
        name="split_panel",
    )(place, mine, other)
    pieces = lax.axis_size("x")
    partial = pl.pallas_call(
        lambda *refs: product_kernel(pieces, *refs),
        out_shape=jax.ShapeDtypeStruct((block_rows // 2, LANES), jnp.float32),
        in_specs=[SMEM] + [VMEM] * 3,
        out_specs=VMEM,
        compiler_params=PARAMS,
        name="multiply",
    )(place, panel, total, mate)
    parts = lax.all_to_all(
        partial.reshape(block_rows // 8, 4, LANES), ("x", "core", "yh", "zq"), split_axis=0, concat_axis=0, tiled=True
    )
    return pl.pallas_call(
        lambda *refs: last_kernel(pieces, *refs),
        out_shape=jax.ShapeDtypeStruct((4, width), jnp.float32),
        in_specs=[VMEM],
        out_specs=VMEM,
        compiler_params=PARAMS,
        name="sum_parts",
    )(parts.reshape(block_rows // 2, LANES))


def solution(mesh):
    fine = Mesh(mesh.devices.reshape(2, 4, 2, 8, 2, 4), ("yh", "zq", "zp", "x", "core", "yl"))
    in_specs = (
        P(("x", "core", "yl"), None),
        P(("x", "core", "yl"), None),
        P(("x", "core", "yl")),
        P(("yh", "zq", "zp"), None, "yl", ("x", "core")),
        P(("yh", "zq", "zp")),
    )
    out_specs = P(("yl", "x", "core", "yh", "zq", "zp"), None)
    return jax.shard_map(per_device, mesh=fine, in_specs=in_specs, out_specs=out_specs, check_vma=False)
```

```python
import math

import jax
import jax.numpy as jnp
from jax import lax
from jax.experimental import pallas as pl
from jax.experimental.pallas import tpu as pltpu
from jax.sharding import Mesh, PartitionSpec as P

POLES = 64
pole_radius = 1.5
weight_scale = 0.3

LANES = 128
SLOTS = 8
VMEM = pl.BlockSpec(memory_space=pltpu.VMEM)
SMEM = pl.BlockSpec(memory_space=pltpu.SMEM)
ANY = pl.BlockSpec(memory_space=pl.ANY)
INPUTS = pltpu.CompilerParams(vmem_limit_bytes=56 * 1024 * 1024)
PARAMS = pltpu.CompilerParams(vmem_limit_bytes=40 * 1024 * 1024)


def iota(shape, axis):
    return lax.broadcasted_iota(jnp.int32, shape, axis)


def pack_kernel(rows_axis, cols_axis, *refs):
    ham, mar, owner, sems = refs[4:]
    out_ref = refs[3]
    share, width = ham.shape
    shift = (share * cols_axis).bit_length() - 1
    copies = [pltpu.make_async_copy(ref, to, sems.at[i]) for i, (ref, to) in enumerate(zip(refs[:3], (ham, mar, owner)))]
    for copy in reversed(copies):
        copy.start()
    copies[2].wait()
    own_r = jnp.broadcast_to(owner[...].astype(jnp.float32), (share, share))
    own_c = jnp.sum(jnp.where(iota((share, share), 0) == iota((share, share), 1), own_r, 0.0), axis=1, keepdims=True)
    own_c = jnp.broadcast_to(own_c, (share, share)).astype(jnp.int32)
    own_r = own_r.astype(jnp.int32)
    same = (own_r >> shift) == (own_c >> shift)
    first, second = iota((share, share), 0), iota((share, share), 1)
    rank_r = jnp.sum(jnp.where(same & (first < second), 1.0, 0.0), axis=0, keepdims=True)
    rank_c = jnp.sum(jnp.where(same & (second < first), 1.0, 0.0), axis=1, keepdims=True)
    slot_r = (own_r[:1] >> shift) * SLOTS + rank_r.astype(jnp.int32)
    slot_c = (own_c[:, :1] >> shift) * SLOTS + rank_c.astype(jnp.int32)
    total = rows_axis * SLOTS
    packer = jnp.where(iota((total, share), 0) == jnp.broadcast_to(slot_r, (total, share)), 1.0, 0.0)
    within = (own_c[:, :1] & ((1 << shift) - 1)) + 1
    labels = jnp.where(
        iota((share, total), 1) == jnp.broadcast_to(slot_c, (share, total)),
        jnp.broadcast_to(within, (share, total)).astype(jnp.float32),
        0.0,
    )
    labels = jnp.sum(labels, axis=0, keepdims=True)
    chunk = 2 * width // LANES * SLOTS + 1
    for target in range(rows_axis * cols_axis):
        base = (target + 1) * chunk - 1
        out_ref[base : base + 1, :] = labels
    for which, ref in enumerate((ham, mar)):
        copies[which].wait()
        packed = jnp.dot(packer, ref[...], precision=lax.Precision.HIGHEST, preferred_element_type=jnp.float32)
        for part in range(width // LANES):
            offset = (which * (width // LANES) + part) * SLOTS
            for row in range(rows_axis):
                tile = packed[row * SLOTS : (row + 1) * SLOTS, part * LANES : (part + 1) * LANES]
                for col in range(cols_axis):
                    base = (row * cols_axis + col) * chunk + offset
                    out_ref[base : base + SLOTS, :] = tile


def split(value):
    high = value.astype(jnp.bfloat16)
    return high, (value - high.astype(jnp.float32)).astype(jnp.bfloat16)


def left_kernel(place_ref, coef_ref, blocks_ref, *out_refs):
    rows, depth = blocks_ref.shape[1:]
    piece = rows // 16
    odd_here = place_ref[2] == 1
    for index in range(16):
        x, core = divmod(index, 2)
        re = blocks_ref[0, index * piece : (index + 1) * piece, :]
        im = blocks_ref[1, index * piece : (index + 1) * piece, :]
        for which in range(2):
            value = (coef_ref[2 * which] * re + coef_ref[2 * which + 1] * im).reshape(piece // 16, 2, 8, depth)
            first, second = value[:, 0], value[:, 1]
            upper = iota(first.shape, 1) < 4
            even = jnp.where(upper, first, pltpu.roll(second, 4, 1)).reshape(piece // 2, depth)
            odd = jnp.where(upper, pltpu.roll(first, 4, 1), second).reshape(piece // 2, depth)
            at = (slice(x * piece // 2, (x + 1) * piece // 2), slice(which * depth, (which + 1) * depth))
            out_refs[core][at] = jnp.where(odd_here, odd, even)
            out_refs[2 + core][at] = jnp.where(odd_here, even, odd)


def pair_kernel(own_ref, other_ref, high_ref, low_ref):
    high_ref[...], low_ref[...] = split(own_ref[...] + other_ref[...])


def store_chunks(out_ref, value):
    pairs = value.shape[0] // 8
    left = value[:, :LANES].reshape(pairs, 8, LANES)
    right = value[:, LANES:].reshape(pairs, 8, LANES)
    upper = iota((pairs, 8, LANES), 1) < 4
    out_ref[:, 0] = jnp.where(upper, left, pltpu.roll(right, 4, 1))
    out_ref[:, 1] = jnp.where(upper, pltpu.roll(left, 4, 1), right)


def multiply(out_ref, which, highs, lows, panel_high_ref, panel_low_ref):
    dot = lambda a, b: jnp.dot(a, b, preferred_element_type=jnp.float32)
    for index in range(2):

        @pl.when(which == index)
        def _():
            high, low, panel = highs[index][...], lows[index][...], panel_high_ref[...]
            store_chunks(out_ref, dot(high, panel) + (dot(low, panel) + dot(high, panel_low_ref[...])))


def first_kernel(senders, place_ref, rows_ref, high0, low0, high1, low1, out_ref, panel_high_ref, panel_low_ref):
    row, core = place_ref[0], place_ref[1]
    chunk = rows_ref.shape[0] // senders
    depth = panel_high_ref.shape[0] // 2
    parts = (chunk - 1) // SLOTS
    labels = rows_ref[pl.ds(chunk - 1, senders, stride=chunk), :]
    lane = iota((senders, LANES), 1)
    wanted = (iota((senders, depth), 1) + 1).astype(jnp.float32)
    places = []
    for slot in range(SLOTS):
        label = jnp.sum(jnp.where(lane == row * SLOTS + slot, labels, 0.0), axis=1, keepdims=True)
        places.append(jnp.where(jnp.broadcast_to(label, (senders, depth)) == wanted, 1.0, 0.0))
    places = jnp.concatenate(places, axis=0).astype(jnp.bfloat16)
    for part in range(parts):
        values = [rows_ref[pl.ds(part * SLOTS + slot, senders, stride=chunk), :] for slot in range(SLOTS)]
        pieces = split(jnp.concatenate(values, axis=0))
        which, left = divmod(part, parts // 2)
        at = (slice(which * depth, (which + 1) * depth), slice(left * LANES, (left + 1) * LANES))
        for ref, piece in zip((panel_high_ref, panel_low_ref), pieces):
            placed = lax.dot_general(places, piece, (((0,), (0,)), ((), ())), preferred_element_type=jnp.float32)
            ref[at] = placed.astype(jnp.bfloat16)
    multiply(out_ref, 1 - core, (high0, high1), (low0, low1), panel_high_ref, panel_low_ref)


def second_kernel(place_ref, high0, low0, high1, low1, panel_high_ref, panel_low_ref, out_ref):
    multiply(out_ref, place_ref[1], (high0, high1), (low0, low1), panel_high_ref, panel_low_ref)


def last_kernel(parts_ref, out_ref):
    total = jnp.sum(parts_ref[...], axis=0)
    out_ref[:, :LANES] = total[:4]
    out_ref[:, LANES:] = total[4:]


def per_device(hamiltonian, margin, owner, inverse_blocks, pole_index):
    rows_axis = lax.axis_size("x") * lax.axis_size("core")
    cols_axis = lax.axis_size("yl")
    share, width = hamiltonian.shape
    senders = rows_axis * cols_axis
    chunk = 2 * width // LANES * SLOTS + 1
    packed = pl.pallas_call(
        lambda *refs: pack_kernel(rows_axis, cols_axis, *refs),
        out_shape=jax.ShapeDtypeStruct((senders * chunk, LANES), jnp.float32),
        in_specs=[ANY] * 3,
        out_specs=VMEM,
        scratch_shapes=[
            pltpu.VMEM((share, width), jnp.float32),
            pltpu.VMEM((share, width), jnp.float32),
            pltpu.VMEM((1, share), jnp.int32),
            pltpu.SemaphoreType.DMA((3,)),
        ],
        compiler_params=INPUTS,
        name="pack_rows",
    )(hamiltonian, margin, owner.reshape(1, share))
    arrived = lax.all_to_all(
        packed.reshape(senders, 1, chunk * LANES), ("x", "core", "yl"), split_axis=0, concat_axis=0, tiled=True
    ).reshape(senders * chunk, LANES)

    theta = math.pi * (pole_index[0].astype(jnp.float32) + 0.5) / POLES
    energy, damping = pole_radius * jnp.cos(theta), pole_radius * jnp.sin(theta)
    weight_re, weight_im = weight_scale * jnp.cos(theta), weight_scale * jnp.sin(theta)
    shifted_re = weight_re * energy - weight_im * damping
    shifted_im = weight_re * damping + weight_im * energy
    coefs = jnp.stack([-weight_im, -weight_re, shifted_im, shifted_re])
    block_rows, depth = inverse_blocks.shape[2:]
    core = lax.axis_index("core")
    place = jnp.stack(
        [lax.axis_index("x") * lax.axis_size("core") + core, core, lax.axis_index("zp")]
    ).astype(jnp.int32)
    factor = jax.ShapeDtypeStruct((block_rows // 4, 2 * depth), jnp.float32)
    factors = pl.pallas_call(
        left_kernel,
        out_shape=(factor,) * 4,
        in_specs=[SMEM, SMEM, VMEM],
        out_specs=(VMEM,) * 4,
        compiler_params=PARAMS,
        cost_estimate=pl.CostEstimate(flops=4 * block_rows * depth, bytes_accessed=16 * block_rows * depth, transcendentals=0),
        name="left_factors",
    )(place, coefs, inverse_blocks[0])
    z_axis = lax.axis_size("zq") * lax.axis_size("zp")
    pairs = (
        [(i, i ^ 1) for i in range(z_axis)],
        [(i, (i - 1 if i % 2 == 0 else i + 1) % z_axis) for i in range(z_axis)],
    )
    part = jax.ShapeDtypeStruct(factor.shape, jnp.bfloat16)
    summed = []
    for own, sent, pair in zip(factors[:2], factors[2:], pairs):
        summed += pl.pallas_call(
            pair_kernel,
            out_shape=(part, part),
            in_specs=[VMEM] * 2,
            out_specs=(VMEM, VMEM),
            compiler_params=PARAMS,
            cost_estimate=pl.CostEstimate(flops=block_rows * depth, bytes_accessed=6 * block_rows * depth, transcendentals=0),
            name="pair_sums",
        )(own, lax.ppermute(sent, ("zq", "zp"), pair))
    chunks = jax.ShapeDtypeStruct((block_rows // 32, 2, 8, LANES), jnp.float32)
    panel = jax.ShapeDtypeStruct((2 * depth, width), jnp.bfloat16)
    sent, panel_high, panel_low = pl.pallas_call(
        lambda *refs: first_kernel(senders, *refs),
        out_shape=(chunks, panel, panel),
        in_specs=[SMEM] + [VMEM] * 5,
        out_specs=(VMEM,) * 3,
        compiler_params=PARAMS,
        name="place_and_multiply",
    )(place, arrived, *summed)
    received = lax.ppermute(sent, "core", [(0, 1), (1, 0)])
    kept = pl.pallas_call(
        second_kernel,
        out_shape=chunks,
        in_specs=[SMEM] + [VMEM] * 6,
        out_specs=VMEM,
        compiler_params=PARAMS,
        cost_estimate=pl.CostEstimate(flops=3 * block_rows * depth * width, bytes_accessed=block_rows * depth * 4, transcendentals=0),
        name="multiply_own",
    )(place, *summed, panel_high, panel_low)
    both = (kept + received).reshape(block_rows // 16, 8, LANES)
    parts = lax.all_to_all(both, ("x", "yh", "zq"), split_axis=0, concat_axis=0, tiled=True)
    return pl.pallas_call(
        last_kernel,
        out_shape=jax.ShapeDtypeStruct((4, width), jnp.float32),
        in_specs=[VMEM],
        out_specs=VMEM,
        compiler_params=PARAMS,
        name="sum_parts",
    )(parts)


def solution(mesh):
    fine = Mesh(mesh.devices.reshape(2, 4, 2, 8, 2, 4), ("yh", "zq", "zp", "x", "core", "yl"))
    in_specs = (
        P(("x", "core", "yl"), None),
        P(("x", "core", "yl"), None),
        P(("x", "core", "yl")),
        P(("yh", "zq", "zp"), None, "yl", ("x", "core")),
        P(("yh", "zq", "zp")),
    )
    out_specs = P(("yl", "x", "core", "yh", "zq", "zp"), None)
    return jax.shard_map(per_device, mesh=fine, in_specs=in_specs, out_specs=out_specs, check_vma=False)
```
